32 devices in a mesh: pix: 8 (over z, x), br: 4 (over y, core).
Axes of the slice: x: 2, y: 2, z: 4, core: 2. Of those that a mesh axis runs over, the one named last changes fastest.
Arguments:
- features: bfloat16 [192, 64, 2048], P('pix'), may hold values from -6 to 6
- branch_weight: bfloat16 [4, 2048, 512], P('br'), may hold values from -0.125 to 0.125
- branch_gain: float32 [4, 512], P('br'), may hold values from 0.5 to 1.5
- branch_shift: float32 [4, 512], P('br'), may hold values from -2 to 2
- trunk_weight: bfloat16 [4, 3, 3, 1024, 512], P('br'), may hold values from -0.03125 to 0.03125
- trunk_gain: float32 [512], replicated, may hold values from 0.5 to 1.5
- trunk_shift: float32 [512], replicated, may hold values from -2 to 2
- class_weight: bfloat16 [512, 150], replicated, may hold values from -0.25 to 0.25
- class_bias: float32 [150], replicated, may hold values from -2 to 2
- heights: int32 [16], replicated, may hold values from 1 to 96, as said below
- logit_grad: bfloat16 [192, 64, 150], P(('pix', 'br')), may hold values from -6 to 6
Outputs:
- logits: bfloat16 [192, 64, 150], P(('pix', 'br'))
- feature_grad: float32 [192, 64, 2048], P('pix', None, 'br')
- branch_weight_grad: float32 [4, 2048, 512], P('br', 'pix')
- branch_gain_grad: float32 [4, 512], P('br')
- branch_shift_grad: float32 [4, 512], P('br')
- trunk_weight_grad: float32 [4, 3, 3, 1024, 512], P('br', None, None, 'pix')
- trunk_gain_grad: float32 [512], P('br')
- trunk_shift_grad: float32 [512], P('br')
- class_weight_grad: float32 [512, 150], P('br')
- class_bias_grad: float32 [150], replicated
The draws below stay inside these ranges and needn't reach their ends.
Inputs may be any that keep to these rules, and one draw needn't show every extreme that they name: The images' heights in canvas rows, top to bottom; every image spans all 64 columns and the heights sum to 192.
All inputs are finite; a program needn't handle non-finite values.
Results may differ from the reference program's by a relative error of at most 0.0077.
Values may be sent and summed in bfloat16 or wider, within the bound.
A program may use at most 256 MiB of HBM per device.

```python
import jax
import jax.numpy as jnp
from jax import lax

CH = 2048
BR_CH = 512
CLASSES = 150
BRANCHES = 4
WIDTH = 64
ROWS = 192
IMAGES = 16
CIN_BLOCK = 1024


def draw_heights(key, part):
    key = jax.random.fold_in(key, 11)
    cut_key = jax.random.fold_in(key, 1)
    order_key = jax.random.fold_in(key, 2)
    tallest = ROWS // 2
    remaining = ROWS - tallest - 1
    order = jax.random.permutation(cut_key, remaining - 1).astype(jnp.int32) + 1
    cuts = jnp.sort(order[:IMAGES - 3]).astype(jnp.int32)
    edges = jnp.concatenate([jnp.zeros((1,), jnp.int32), cuts, jnp.full((1,), remaining, jnp.int32)])
    others = (edges[1:] - edges[:-1]).astype(jnp.int32)
    values = jnp.concatenate([jnp.full((1,), tallest, jnp.int32), jnp.ones((1,), jnp.int32), others])
    places = jax.random.permutation(order_key, IMAGES).astype(jnp.int32)
    return values[places].astype(jnp.int32)


def level_of(stream_key, extent, pieces, smallest, high):
    loudness, own = 1.0, jax.random.fold_in(stream_key, 6)
    for axis_at, blocks in pieces:
        draws = jnp.exp(jax.random.uniform(jax.random.fold_in(own, axis_at), (blocks,), jnp.float32, smallest / len(pieces), high / len(pieces)))
        loudness = loudness * jnp.repeat(draws, extent[axis_at] // blocks).reshape([-1 if axis == axis_at else 1 for axis in range(len(extent))])
    return loudness


def gaussian(stream_key, extent, scale, most, cuts=(), kind=jnp.bfloat16):
    values = jax.random.normal(stream_key, extent, jnp.float32) * scale
    if len(cuts) > 0:
        values = level_of(stream_key, extent, cuts, -0.22, 0.18) * values
    return jnp.clip(values, min=-most, max=most).astype(kind)


def setup_inputs(seed: int = 0) -> dict:
    splits = jax.random.split(jax.random.key(seed), 12)
    features = gaussian(splits[0], (ROWS, WIDTH, CH), 1.0, 6.0, ((0, 8),))
    branch_weight = gaussian(splits[1], (BRANCHES, CH, BR_CH), CH ** -0.5, 0.125, ((0, 4),))
    branch_gain = jnp.clip(1.0 + 0.1 * jax.random.normal(splits[2], (BRANCHES, BR_CH), jnp.float32), 0.5, 1.5)
    branch_shift = gaussian(splits[3], (BRANCHES, BR_CH), 0.5, 2.0, ((0, 4),), jnp.float32)
    trunk_weight = gaussian(splits[4], (BRANCHES, 3, 3, CIN_BLOCK, BR_CH), (9 * CIN_BLOCK * BRANCHES) ** -0.5, 0.03125, ((0, 4),))
    trunk_gain = jnp.clip(1.0 + 0.1 * jax.random.normal(splits[5], (BR_CH,), jnp.float32), 0.5, 1.5)
    trunk_shift = gaussian(splits[6], (BR_CH,), 0.5, 2.0, (), jnp.float32)
    class_weight = gaussian(splits[7], (BR_CH, CLASSES), BR_CH ** -0.5, 0.25)
    class_bias = gaussian(splits[8], (CLASSES,), 0.5, 2.0, (), jnp.float32)
    heights = draw_heights(jax.random.fold_in(splits[11], 71), 0)
    logit_grad = gaussian(splits[10], (ROWS, WIDTH, CLASSES), 1.0, 6.0, ((0, 32),))
    return dict(features=features, branch_weight=branch_weight, branch_gain=branch_gain, branch_shift=branch_shift, trunk_weight=trunk_weight, trunk_gain=trunk_gain, trunk_shift=trunk_shift, class_weight=class_weight, class_bias=class_bias, heights=heights, logit_grad=logit_grad)


@jax.custom_vjp
def low(v):
    return lax.optimization_barrier(v.astype(jnp.bfloat16)).astype(jnp.float32)

@jax.custom_vjp
def low_back(v):
    return v

def low_keep(v):
    return (low(v), None)

def low_pass(kept, grad):
    return (grad,)

def back_keep(v):
    return (v, None)

def back_low(kept, grad):
    return (low(grad),)
low.defvjp(low_keep, low_pass)
low_back.defvjp(back_keep, back_low)
bin_sides = (1, 2, 3, 6)
norm_eps = 1e-05

def activate(value):
    return jax.nn.gelu(value, approximate=True)

def exact_dot(left, right):
    return jnp.dot(left, right, precision=lax.Precision.HIGHEST, preferred_element_type=jnp.float32)

def image_of(starts, row_ids):
    return (lax.optimization_barrier(jnp.sum((starts[None, :] <= row_ids[:, None]).astype(jnp.int32), axis=1)) - 1).astype(jnp.int32)

def geometry(heights, side):
    starts = (jnp.cumsum(heights) - heights).astype(jnp.int32)
    row_ids = jnp.arange(ROWS, dtype=jnp.int32)
    image = image_of(starts, row_ids)
    height = heights[image].astype(jnp.int32)
    place = (row_ids - starts[image]).astype(jnp.int32)
    bin_ids = jnp.arange(side, dtype=jnp.int32)
    lower = bin_ids[None, :] * height[:, None] // side
    upper = ((bin_ids[None, :] + 1) * height[:, None] + side - 1) // side
    member = (place[:, None] >= lower) & (place[:, None] < upper)
    owner = image[None, :] == jnp.arange(IMAGES, dtype=jnp.int32)[:, None]
    row_hot = (owner[:, None, :] & member.T[None, :, :]).reshape(IMAGES * side, ROWS).astype(jnp.float32)
    image_low = bin_ids[None, :] * heights[:, None] // side
    image_up = ((bin_ids[None, :] + 1) * heights[:, None] + side - 1) // side
    col_ids = jnp.arange(WIDTH, dtype=jnp.int32)
    col_low = bin_ids * WIDTH // side
    col_up = ((bin_ids + 1) * WIDTH + side - 1) // side
    col_mask = ((col_ids[None, :] >= col_low[:, None]) & (col_ids[None, :] < col_up[:, None])).astype(jnp.float32)
    counts = ((image_up - image_low)[:, :, None] * (col_up - col_low)[None, None, :]).astype(jnp.float32)
    numer = (2 * place + 1) * side - height
    ahead = numer >= 0
    first = jnp.where(ahead, numer // (2 * height), 0).astype(jnp.int32)
    frac = jnp.where(ahead, (numer - 2 * height * first).astype(jnp.float32) / (2 * height).astype(jnp.float32), 0.0)
    second = jnp.minimum(first + 1, side - 1).astype(jnp.int32)
    col_numer = (2 * col_ids + 1) * side - WIDTH
    col_ahead = col_numer >= 0
    col_first = jnp.where(col_ahead, col_numer // (2 * WIDTH), 0).astype(jnp.int32)
    col_frac = jnp.where(col_ahead, (col_numer - 2 * WIDTH * col_first).astype(jnp.float32) / (2.0 * WIDTH), 0.0)
    col_second = jnp.minimum(col_first + 1, side - 1).astype(jnp.int32)
    col_weight = (1.0 - col_frac)[:, None] * (bin_ids[None, :] == col_first[:, None]).astype(jnp.float32)
    col_weight = col_weight + col_frac[:, None] * (bin_ids[None, :] == col_second[:, None]).astype(jnp.float32)
    return (row_hot, counts, col_mask, image, first, second, frac, col_weight)

def forward(features, branch_weight, branch_gain, branch_shift, trunk_weight, trunk_gain, trunk_shift, class_weight, class_bias, geoms, image_ids):
    total_rows, width, channels = features.shape
    slice_width = channels // BRANCHES
    flat = features.reshape(total_rows * width, channels)
    blocks = []
    for branch_at in range(BRANCHES):
        side = bin_sides[branch_at]
        row_hot, counts, col_mask, image, first, second, frac, col_weight = geoms[branch_at]
        proj = low_back(exact_dot(flat, branch_weight[branch_at]).reshape(total_rows, width, -1))
        col_sum = jnp.einsum('jx,rxc->rjc', col_mask, proj, precision=lax.Precision.HIGHEST)
        sums = exact_dot(row_hot, col_sum.reshape(total_rows, -1)).reshape(IMAGES, side, side, -1)
        pooled = sums / counts[..., None]
        centre = lax.optimization_barrier(jnp.mean(pooled, axis=(0, 1, 2)))
        centred = pooled - centre
        spread = lax.optimization_barrier(jnp.mean(centred * centred, axis=(0, 1, 2)))
        normed = centred * lax.rsqrt(spread + norm_eps) * branch_gain[branch_at] + branch_shift[branch_at]
        active = activate(normed).reshape(IMAGES * side, side, -1)
        row_mix = (1.0 - frac)[:, None, None] * active[image * side + first] + frac[:, None, None] * active[image * side + second]
        upsampled = low(jnp.einsum('xj,rjc->rxc', col_weight, row_mix, precision=lax.Precision.HIGHEST))
        own_slice = features[:, :, branch_at * slice_width:(branch_at + 1) * slice_width]
        blocks.append(jnp.concatenate([own_slice, upsampled], axis=2))
    edge = jnp.full((1,), -1, jnp.int32)
    image_pad = jnp.concatenate([edge, image_ids, edge])
    summed = jnp.zeros((total_rows * width, trunk_weight.shape[-1]), jnp.float32)
    for branch_at in range(BRANCHES):
        padded = jnp.pad(blocks[branch_at], ((1, 1), (1, 1), (0, 0)))
        in_width = padded.shape[2]
        for row_step in (-1, 0, 1):
            keep = (image_pad[1 + row_step:1 + row_step + total_rows] == image_ids).astype(jnp.float32)
            band = padded[1 + row_step:1 + row_step + total_rows] * keep[:, None, None]
            for col_step in (-1, 0, 1):
                window = band[:, 1 + col_step:1 + col_step + width].reshape(-1, in_width)
                summed = summed + exact_dot(window, trunk_weight[branch_at, row_step + 1, col_step + 1])
    summed = low_back(summed.reshape(total_rows, width, -1))
    t_mean = lax.optimization_barrier(jnp.mean(summed, axis=(0, 1)))
    t_var = lax.optimization_barrier(jnp.mean(summed * summed, axis=(0, 1))) - t_mean * t_mean
    t_hat = (summed - t_mean) * lax.rsqrt(t_var + norm_eps)
    hidden = low(activate(t_hat * trunk_gain + trunk_shift))
    return jnp.einsum('rxc,ck->rxk', hidden, class_weight, precision=lax.Precision.HIGHEST) + class_bias

def reference(features, branch_weight, branch_gain, branch_shift, trunk_weight, trunk_gain, trunk_shift, class_weight, class_bias, heights, logit_grad):
    geoms = tuple((geometry(heights, side) for side in bin_sides))
    image_ids = geoms[0][3]
    floats = tuple((arr.astype(jnp.float32) for arr in (features, branch_weight, branch_gain, branch_shift, trunk_weight, trunk_gain, trunk_shift, class_weight, class_bias)))

    def run(*params):
        return forward(*params, geoms, image_ids)
    logits, pull = jax.vjp(run, *floats)
    grads = pull(logit_grad.astype(jnp.float32))
    return (logits.astype(jnp.bfloat16), grads[0], grads[1], grads[2], grads[3], grads[4], grads[5], grads[6], grads[7], grads[8])
```

```python
import functools

import jax
import jax.numpy as jnp
import numpy as np
from jax import lax
from jax.experimental import pallas as pl
from jax.experimental.pallas import tpu as pltpu
from jax.sharding import PartitionSpec as P

bin_sides = (1, 2, 3, 6)
norm_eps = 1e-05


def padded_2(cells, sides, width):
    for axis, dim in sides:
        count = lax.axis_size(axis)
        ends = count - 1
        head = lax.slice_in_dim(cells, 0, width, axis=dim)
        tail = lax.slice_in_dim(cells, cells.shape[dim] - width, cells.shape[dim], axis=dim)
        cells = jnp.concatenate(
            [
                lax.ppermute(tail, axis, [(i, (i + 1) % count) for i in range(ends)]),
                cells,
                lax.ppermute(head, axis, [((i + 1) % count, i) for i in range(ends)]),
            ],
            axis=dim,
        )
    return cells


def activate(value):
    return jax.nn.gelu(value, approximate=True)


def gelu_slope(value):
    unused, pull = jax.vjp(activate, value)
    return pull(jnp.ones_like(value))[0]


def image_of(starts, row_ids):
    return jnp.sum((starts[None, :] <= row_ids[:, None]).astype(jnp.int32), axis=1) - 1


def exact_dot(left, right):
    return jnp.dot(left, right, precision=lax.Precision.HIGHEST, preferred_element_type=jnp.float32)


def contract(left, right, left_dim, right_dim):
    return lax.dot_general(
        left, right, (((left_dim,), (right_dim,)), ((), ())), preferred_element_type=jnp.float32
    )


def row_columns(sides, width, most_side):
    out = np.zeros((len(sides), width, most_side), np.float32)
    for b, side in enumerate(sides):
        for x in range(width):
            numer = (2 * x + 1) * side - width
            first = numer // (2 * width) if numer >= 0 else 0
            frac = (numer - 2 * width * first) / (2.0 * width) if numer >= 0 else 0.0
            second = min(first + 1, side - 1)
            out[b, x, first] += 1.0 - frac
            out[b, x, second] += frac
    return out


def shifted_columns(sides, width, most_side):
    cols = row_columns(sides, width, most_side)
    out = np.zeros((len(sides), 3, width, most_side), np.float32)
    for at, step in enumerate((-1, 0, 1)):
        for x in range(width):
            if 0 <= x + step < width:
                out[:, at, x] = cols[:, x + step]
    return out


def column_bins(sides, width, most_side):
    out = np.zeros((len(sides), most_side, width), np.float32)
    for b, side in enumerate(sides):
        for j in range(side):
            out[b, j, j * width // side : ((j + 1) * width + side - 1) // side] = 1.0
    return out


def split_dot(left, right, **kw):
    high = left.astype(jnp.bfloat16)
    low = (left - high.astype(jnp.float32)).astype(jnp.bfloat16)
    return jnp.dot(high, right, preferred_element_type=jnp.float32) + jnp.dot(
        low, right, preferred_element_type=jnp.float32
    )


def on_device(
    features,
    branch_weight,
    branch_gain,
    branch_shift,
    trunk_weight,
    trunk_gain,
    trunk_shift,
    class_weight,
    class_bias,
    heights,
    logit_grad,
):
    rows_dev, width, channels = features.shape
    branch_ch = branch_weight.shape[2]
    classes = class_weight.shape[1]
    images = heights.shape[0]
    most_side = max(bin_sides)
    pix_count = lax.axis_size("pix")
    br_count = lax.axis_size("br")
    pix_at = lax.axis_index("pix")
    br_at = lax.axis_index("br")
    own_rows = rows_dev // br_count
    total_pix = float(rows_dev * width * pix_count)
    slice_width = channels // br_count
    bf16 = jnp.bfloat16
    side = jnp.sum(jnp.where(jnp.arange(len(bin_sides)) == br_at, jnp.array(bin_sides, jnp.int32), 0))
    starts = jnp.cumsum(heights) - heights
    bin_ids = jnp.arange(most_side, dtype=jnp.int32)
    in_use = bin_ids < side
    ext_ids = pix_at * rows_dev - 1 + jnp.arange(rows_dev + 2, dtype=jnp.int32)
    on_canvas = (ext_ids >= 0) & (ext_ids < rows_dev * pix_count)
    ext_image = jnp.where(on_canvas, image_of(starts, ext_ids), -1)
    owner = ext_image[:, None] == jnp.arange(images, dtype=jnp.int32)[None, :]
    height = jnp.maximum(jnp.sum(jnp.where(owner, heights[None, :], 0), axis=1), 1)
    place = ext_ids - jnp.sum(jnp.where(owner, starts[None, :], 0), axis=1)
    lower = bin_ids[None, :] * height[:, None] // side
    upper = ((bin_ids[None, :] + 1) * height[:, None] + side - 1) // side
    member = in_use[None, :] & (place[:, None] >= lower) & (place[:, None] < upper)
    row_hot = (
        (owner.T[:, None, :] & member.T[None, :, :])
        .reshape(images * most_side, rows_dev + 2)[:, 1:-1]
        .astype(jnp.float32)
    )
    numer = (2 * place + 1) * side - height
    ahead = numer >= 0
    first = jnp.where(ahead, numer // (2 * height), 0)
    frac = jnp.where(
        ahead,
        (numer - 2 * height * first).astype(jnp.float32) / (2 * height).astype(jnp.float32),
        0.0,
    )
    second = jnp.minimum(first + 1, side - 1)
    mix = (bin_ids[:, None] == first[None, :]).astype(jnp.float32) * (1.0 - frac)[None, :]
    mix = mix + (bin_ids[:, None] == second[None, :]).astype(jnp.float32) * frac[None, :]
    interp = (owner.T.astype(jnp.float32)[:, None, :] * mix[None]).reshape(
        images * most_side, rows_dev + 2
    )
    image_low = bin_ids[None, :] * heights[:, None] // side
    image_up = ((bin_ids[None, :] + 1) * heights[:, None] + side - 1) // side
    col_low = bin_ids * width // side
    col_up = ((bin_ids + 1) * width + side - 1) // side
    valid = in_use[:, None] & in_use[None, :]
    counts = jnp.where(
        valid[None], (image_up - image_low)[:, :, None] * (col_up - col_low)[None, None, :], 1
    ).astype(jnp.float32)
    valid_f = valid.astype(jnp.float32)[None, :, :, None]
    all_cols = jnp.asarray(shifted_columns(bin_sides, width, most_side))
    all_bins = jnp.asarray(column_bins(bin_sides, width, most_side), bf16)
    own_bins = lax.dynamic_index_in_dim(all_bins, br_at, 0, False)

    col_feat = jnp.einsum("jx,rxc->jrc", own_bins, features, preferred_element_type=jnp.float32)
    col_proj = split_dot(col_feat.reshape(-1, channels), branch_weight[0])
    col_proj = col_proj.reshape(most_side, rows_dev, branch_ch)
    pool_part = jnp.einsum("nr,jrc->njc", row_hot, col_proj, precision=lax.Precision.HIGHEST)
    sums = lax.psum(pool_part, "pix").reshape(images, most_side, most_side, branch_ch)
    pooled = sums / counts[..., None]
    total_bins = (images * side * side).astype(jnp.float32)
    centre = jnp.sum(pooled * valid_f, axis=(0, 1, 2)) / total_bins
    centred = (pooled - centre) * valid_f
    b_inv = lax.rsqrt(jnp.sum(centred * centred, axis=(0, 1, 2)) / total_bins + norm_eps)
    b_hat = centred * b_inv
    normed = b_hat * branch_gain[0] + branch_shift[0]
    active = (activate(normed) * valid_f).reshape(images * most_side, most_side, branch_ch)
    row_mix = jnp.einsum("nr,njc->rjc", interp, active, precision=lax.Precision.HIGHEST).astype(bf16)

    def keep(step):
        return (ext_image[1 + step : 1 + step + rows_dev] == ext_image[1:-1]).astype(bf16)

    own_slice = lax.dynamic_slice_in_dim(features, br_at * slice_width, slice_width, 2)
    feat_ext = padded_2(own_slice, (("pix", 0),), 1)
    feat_pad = jnp.pad(feat_ext, ((0, 0), (1, 1), (0, 0)))
    feat_weight = trunk_weight[0, :, :, :slice_width]
    up_weight = trunk_weight[0, :, :, slice_width:]
    feat_sum = jnp.zeros((rows_dev * width, branch_ch), jnp.float32)
    up_sum = [jnp.zeros((rows_dev * most_side, branch_ch), jnp.float32) for _ in range(3)]
    for at in range(3):
        band = feat_pad[at : at + rows_dev] * keep(at - 1)[:, None, None]
        up_band = (row_mix[at : at + rows_dev] * keep(at - 1)[:, None, None]).reshape(-1, branch_ch)
        for to in range(3):
            window = band[:, to : to + width].reshape(-1, slice_width)
            feat_sum = feat_sum + jnp.dot(
                window, feat_weight[at, to], preferred_element_type=jnp.float32
            )
            up_sum[to] = up_sum[to] + jnp.dot(
                up_band, up_weight[at, to], preferred_element_type=jnp.float32
            )
    pre = lax.psum_scatter(
        feat_sum.astype(bf16).reshape(rows_dev, width, branch_ch), "br", scatter_dimension=0, tiled=True
    ).astype(jnp.float32)
    up_all = jnp.stack(up_sum).reshape(3, br_count, own_rows, most_side, branch_ch).astype(bf16)
    up_all = lax.all_to_all(up_all, "br", 1, 0, tiled=False)
    pre = pre + jnp.einsum(
        "btxj,btrjc->rxc", all_cols.astype(bf16), up_all, preferred_element_type=jnp.float32
    )

    both = ("pix", "br")
    first_sum, square_sum = lax.psum((jnp.sum(pre, (0, 1)), jnp.sum(pre * pre, (0, 1))), both)
    t_mean = first_sum / total_pix
    t_inv = lax.rsqrt(square_sum / total_pix - t_mean * t_mean + norm_eps)
    t_hat = (pre - t_mean) * t_inv
    t_norm = t_hat * trunk_gain + trunk_shift
    hidden = activate(t_norm).astype(bf16).reshape(-1, branch_ch)
    logits = jnp.dot(hidden, class_weight, preferred_element_type=jnp.float32) + class_bias
    logits = logits.reshape(own_rows, width, classes).astype(bf16)
    grad_flat = logit_grad.reshape(-1, classes)
    weight_part = contract(hidden, grad_flat, 0, 0)
    bias_part = jnp.sum(grad_flat.astype(jnp.float32), axis=0)
    d_norm = contract(grad_flat, class_weight, 1, 1).reshape(pre.shape) * gelu_slope(t_norm)
    gain_part, shift_part, bias_part = lax.psum(
        (jnp.sum(d_norm * t_hat, (0, 1)), jnp.sum(d_norm, (0, 1)), bias_part), both
    )
    weight_part = lax.psum(lax.psum_scatter(weight_part, "br", scatter_dimension=0, tiled=True), "pix")
    d_pre = (
        trunk_gain * t_inv * (d_norm - shift_part / total_pix - t_hat * gain_part / total_pix)
    ).astype(bf16)

    d_cols = jnp.einsum(
        "btxj,rxc->btrjc", all_cols.astype(bf16), d_pre, preferred_element_type=jnp.float32
    ).astype(bf16)
    d_cols = lax.all_to_all(d_cols, "br", 0, 2, tiled=True)[0]
    d_mix = jnp.zeros((rows_dev + 2, most_side, branch_ch), jnp.float32)
    up_taps = []
    for at in range(3):
        part = jnp.zeros((rows_dev * most_side, branch_ch), jnp.float32)
        kept = d_cols * keep(at - 1)[None, :, None, None]
        up_band = row_mix[at : at + rows_dev].reshape(-1, branch_ch)
        for to in range(3):
            part = part + contract(kept[to].reshape(-1, branch_ch), up_weight[at, to], 1, 1)
            up_taps.append(contract(up_band, kept[to].reshape(-1, branch_ch), 0, 0))
        d_mix = d_mix.at[at : at + rows_dev].add(part.reshape(rows_dev, most_side, branch_ch))
    d_bin_part = jnp.einsum("nr,rjc->njc", interp, d_mix, precision=lax.Precision.HIGHEST)
    d_active = lax.psum(d_bin_part, "pix").reshape(images, most_side, most_side, branch_ch)
    d_normed = d_active * valid_f * gelu_slope(normed)
    branch_gain_part = jnp.sum(d_normed * b_hat, axis=(0, 1, 2))
    branch_shift_part = jnp.sum(d_normed, axis=(0, 1, 2))
    d_pooled = (
        branch_gain[0]
        * b_inv
        * (d_normed - branch_shift_part / total_bins - b_hat * branch_gain_part / total_bins)
        * valid_f
    )
    d_sums = (d_pooled / counts[..., None]).reshape(images * most_side, most_side, branch_ch)

    d_all = lax.all_gather(d_pre, "br", axis=0, tiled=True)
    d_pad = jnp.pad(padded_2(d_all, (("pix", 0),), 1), ((0, 0), (1, 1), (0, 0)))
    d_flat = d_all.reshape(-1, branch_ch)
    d_own = jnp.zeros((rows_dev * width, slice_width), jnp.float32)
    feat_taps = []
    for at in range(3):
        band = feat_pad[at : at + rows_dev] * keep(at - 1)[:, None, None]
        back = d_pad[2 - at : 2 - at + rows_dev] * keep(1 - at)[:, None, None]
        for to in range(3):
            window = band[:, to : to + width].reshape(-1, slice_width)
            feat_taps.append(contract(window, d_flat, 0, 0))
            source = back[:, 2 - to : 2 - to + width].reshape(-1, branch_ch)
            d_own = d_own + contract(source, feat_weight[at, to], 1, 1)
    taps = jnp.concatenate([jnp.stack(feat_taps), jnp.stack(up_taps)], axis=1).astype(bf16)
    trunk_weight_grad = lax.psum_scatter(taps, "pix", scatter_dimension=1, tiled=True)
    trunk_weight_grad = trunk_weight_grad.astype(jnp.float32).reshape(1, 3, 3, -1, branch_ch)

    d_col = jnp.einsum("nr,njc->jrc", row_hot, d_sums, precision=lax.Precision.HIGHEST).astype(bf16)
    spread = contract(d_col.reshape(-1, branch_ch), branch_weight[0], 1, 1).astype(bf16)
    spread = spread.reshape(1, most_side, rows_dev, br_count, slice_width)
    spread = lax.all_to_all(spread, "br", 3, 0, tiled=False)[:, 0]
    feature_grad = jnp.einsum(
        "bjx,bjrc->rxc", all_bins, spread, preferred_element_type=jnp.float32
    ) + d_own.reshape(rows_dev, width, slice_width)
    branch_term = contract(col_feat.astype(bf16).reshape(-1, channels), d_col.reshape(-1, branch_ch), 0, 0)
    branch_weight_grad = lax.psum_scatter(branch_term, "pix", scatter_dimension=0, tiled=True)[None]
    start = br_at * (branch_ch // br_count)
    return (
        logits,
        feature_grad,
        branch_weight_grad,
        branch_gain_part[None],
        branch_shift_part[None],
        trunk_weight_grad,
        lax.dynamic_slice_in_dim(gain_part, start, branch_ch // br_count, 0),
        lax.dynamic_slice_in_dim(shift_part, start, branch_ch // br_count, 0),
        weight_part,
        bias_part,
    )


MESH = pl.DeviceIdType.MESH
HIGH = lax.Precision.HIGHEST
F32 = jnp.float32
BF16 = jnp.bfloat16


def mod2(value, by):
    return lax.bitwise_and(value, jnp.full_like(value, by - 1))


def div2(value, by):
    return lax.shift_right_logical(value, jnp.full_like(value, by.bit_length() - 1))


def dot(left, right):
    return jnp.dot(left, right, preferred_element_type=F32)


def dot_nt(left, right):
    return lax.dot_general(left, right, (((1,), (1,)), ((), ())), preferred_element_type=F32)


def dot_tn(left, right):
    return lax.dot_general(left, right, (((0,), (0,)), ((), ())), preferred_element_type=F32)


def gelu_parts(value):
    inner = 0.7978845608 * (value + 0.044715 * value * value * value)
    tanh = jnp.tanh(inner)
    half = 0.5 * (1.0 + tanh)
    slope = half + 0.5 * value * (1.0 - tanh * tanh) * (
        0.7978845608 * (1.0 + 0.134145 * value * value)
    )
    return value * half, slope


class Shape:
    def __init__(self, features, branch_weight, class_weight, heights, pix, br):
        self.rows, self.width, self.channels = features.shape
        self.ch = branch_weight.shape[2]
        self.classes = class_weight.shape[1]
        self.images = heights.shape[0]
        self.pix, self.br = pix, br
        self.side = max(bin_sides)
        self.bins = self.side * self.images
        self.own = self.rows // br
        self.px = self.rows * self.width
        self.own_px = self.own * self.width
        self.all_rows = self.rows * pix


def fused_kernel(
    d,
    feat_hbm, bw_hbm, tw_hbm, x_hbm, xt_hbm, pool_hbm, spread_hbm,
    bgain, bshift, tgain, tshift, cweight_t, cbias, lgrad, heights,
    logits_out, fg_hbm, bwg_out, twg_hbm, cwg_out, small_out,
    fext, shifted, fgrp, wb, twf, twu, xc, xt, pool8, spread8,
    fc_hi, zsend, zrecv, fcrecv, pfsend, pfrecv, hidden,
    hot_all, mix_all, mix_t, hot_own, mrow, mrow2, mgrp,
    bhat, bnorm, binv, rmsend, rmrecv, actsend, actrecv, hsend, hrecv,
    st1, st2, st3, st4, sr1, sr2, sr3, sr4, tot,
    cwp, lgp, cwsend, cwr1, cw2, cwr2, cw3, cwr3,
    dpext, dpext2, drecv, drsend, drrecv, dwrecv, dssend, dsrecv, smsend, smrecv, ds_all,
    fp_all, fp_t, esend, erecv, fg, keep, sendx, recvz, upsend, uprecv, eye,
    load_sem, out_sem, twg_sem, halo_sem, z_sem, fc_sem, pf_sem, rm_sem, act_sem, h_sem,
    st_sem1, st_sem2, st_sem3, st_sem4, cw_sem1, cw_sem2, cw_sem3,
    dp_sem, dphalo_sem, dp2_sem, dphalo2_sem, fp_sem, dr_sem, dw_sem, ds_sem, sm_sem, e_sem, zz_sem, a_sem, up_sem,
):
    W, C, J, NB, P, B = d.width, d.ch, d.side, d.bins, d.pix, d.br
    PX, OPX, R, Q = d.px, d.own_px, d.rows, d.own
    HJ = J // 2
    lhs_rows = 8 * B * J
    pre = fg.at[pl.ds(3 * lhs_rows, OPX)]
    dnorm = fg.at[pl.ds(3 * lhs_rows + OPX, OPX)]
    p = lax.axis_index("pix")
    b = lax.axis_index("br")
    x_at = lax.rem(p, 2)
    z_at = lax.div(p, 2)
    x_peer = p + 1 - 2 * x_at
    core_peer = b + 1 - 2 * lax.rem(b, 2)
    y_peer = lax.rem(b + 2, B)
    side = jnp.where(b == 0, 1, jnp.where(b == 1, 2, jnp.where(b == 2, 3, 6)))
    side_f = side.astype(F32)

    def remote(src, dst, sem, at, axis, peer):
        return pltpu.make_async_remote_copy(
            src_ref=src, dst_ref=dst, send_sem=sem.at[0, at], recv_sem=sem.at[1, at],
            device_id={axis: peer}, device_id_type=MESH,
        )

    def exchange(axis, sem, src_of, dst_of):
        count, me = (P, p) if axis == "pix" else (B, b)
        copies = []
        for step in range(1, count):
            peer = lax.rem(me + step, count)
            copy = remote(src_of(peer), dst_of(me), sem, step - 1, axis, peer)
            copy.start()
            copies.append(copy)
        return copies

    def arrive(copies):
        for copy in copies:
            copy.wait_recv()

    pending = []

    own_lanes = pl.ds(pl.multiple_of(b * C, C), C)
    groups = R // 8
    gpx = 8 * W
    loads = {}

    def load(name, at, src, dst):
        loads[name] = pltpu.make_async_copy(src, dst, load_sem.at[at])
        loads[name].start()

    load("pool", 0, pool_hbm.at[b], pool8)
    for g in range(groups):
        load(f"feat{g}", 1 + g, feat_hbm.at[pl.ds(g * gpx, gpx)], fgrp.at[g])
    load("wb", 4, bw_hbm, wb)

    barrier = pltpu.get_barrier_semaphore()
    for step in range(1, P):
        pl.semaphore_signal(barrier, inc=1, device_id={"pix": lax.rem(p + step, P)}, device_id_type=MESH)
    for step in range(1, B):
        pl.semaphore_signal(barrier, inc=1, device_id={"br": lax.rem(b + step, B)}, device_id_type=MESH)

    for step in range(1, B):
        for to in (p + 1, p + P - 1, p + 2, p + P - 2):
            pl.semaphore_signal(
                barrier, inc=1, device_id={"pix": lax.rem(to, P), "br": lax.rem(b + step, B)},
                device_id_type=MESH,
            )

    tall = [heights[g] for g in range(d.images)]
    starts = [jnp.int32(0)]
    for g in range(d.images - 1):
        starts.append(starts[-1] + tall[g])

    def row_info(t):
        image = jnp.full(t.shape, -1, jnp.int32)
        height = jnp.ones(t.shape, jnp.int32)
        start = jnp.zeros(t.shape, jnp.int32)
        for g in range(d.images):
            reached = t >= starts[g]
            image = jnp.where(reached, g, image)
            height = jnp.where(reached, tall[g], height)
            start = jnp.where(reached, starts[g], start)
        image = jnp.where(t >= d.all_rows, -2, image)
        return image, height.astype(F32), (t - start).astype(F32)

    def bin_index(shape, axis):
        n = lax.broadcasted_iota(jnp.int32, shape, axis)
        return mod2(n, d.images), div2(n, d.images)

    def floor_div(a, by):
        return jnp.floor((a + 0.5) / by)

    def row_hot(t, g, i):
        image, height, place = row_info(t)
        i_f = i.astype(F32)
        lower = floor_div(i_f * height, side_f)
        upper = floor_div((i_f + 1.0) * height + (side_f - 1.0), side_f)
        inside = (image == g) & (i < side) & (place >= lower) & (place < upper)
        return jnp.where(inside, 1.0, 0.0)

    def row_mix(t, g, i, image_at=None):
        image, height, place = row_info(t)
        twice = 2.0 * height
        numer = (2.0 * place + 1.0) * side_f - height
        first = jnp.where(numer >= 0.0, floor_div(numer, twice), 0.0)
        frac = jnp.where(numer >= 0.0, (numer - twice * first) / twice, 0.0)
        second = jnp.minimum(first + 1.0, side_f - 1.0)
        i_f = i.astype(F32)
        value = jnp.where(i_f == first, 1.0 - frac, 0.0) + jnp.where(i_f == second, frac, 0.0)
        value = jnp.where(image == g, value, 0.0)
        if image_at is not None:
            value = jnp.where(image == image_at, value, 0.0)
        return value

    def halo_rows(shape, axis, first):
        n = lax.broadcasted_iota(jnp.int32, shape, axis)
        k, owner, dev = mod2(n, 8), mod2(div2(n, 8), B), div2(n, 8 * B)
        return first + dev * R + owner * Q + k, k

    g_col, i_col = bin_index((NB, 1), 0)
    g_row, i_row = bin_index((1, NB), 1)
    t_row = lax.broadcasted_iota(jnp.int32, (1, d.all_rows), 1)
    hot_all[...] = row_hot(t_row, g_col, i_col)
    t_own = lax.broadcasted_iota(jnp.int32, (R, 1), 0) + p * R
    hot_own[...] = row_hot(t_own, g_row, i_row)
    t_halo, _ = halo_rows((8 * B * P, 1), 0, -1)
    mix_all[...] = row_mix(t_halo, g_row, i_row)
    t_halo, _ = halo_rows((1, 8 * B * P), 1, -1)
    mix_t[...] = row_mix(t_halo, g_col, i_col)
    t_own = lax.broadcasted_iota(jnp.int32, (32, 128), 0) + p * R
    here = row_info(t_own)[0]
    t_peer = lax.broadcasted_iota(jnp.int32, (32, 128), 0) + x_peer * R
    here_peer = row_info(t_peer)[0]
    t_grp, k_grp = halo_rows((8 * B, 128), 0, p * R)
    here_grp = row_info(t_grp)[0]
    for at, step in enumerate((-1, 1)):
        mrow2[at] = jnp.where(row_info(t_peer + step)[0] == here_peer, 1.0, 0.0)
        mrow[at] = jnp.where(row_info(t_own + step)[0] == here, 1.0, 0.0)
        mgrp[at] = jnp.where((row_info(t_grp + step)[0] == here_grp) & (k_grp < Q), 1.0, 0.0)

    tall_col = jnp.ones((NB, 1), F32)
    for g in range(d.images):
        tall_col = jnp.where(g_col == g, tall[g].astype(F32), tall_col)
    i_f = i_col.astype(F32)
    row_count = floor_div((i_f + 1.0) * tall_col + (side_f - 1.0), side_f) - floor_div(
        i_f * tall_col, side_f
    )
    lane = lax.broadcasted_iota(jnp.int32, (1, HJ * 128), 1)
    j_lane = div2(lane, 128) + jnp.where(mod2(lane, 128) >= 64, HJ, 0)
    j_f = j_lane.astype(F32)
    col_count = floor_div((j_f + 1.0) * W + (side_f - 1.0), side_f) - floor_div(j_f * W, side_f)
    valid = (i_col < side) & (j_lane < side)
    valid_f = jnp.where(valid, 1.0, 0.0)
    count = jnp.where(valid, row_count * col_count, 1.0)
    total_bins = side_f * side_f * float(d.images)

    square = lax.broadcasted_iota(jnp.int32, (C, C), 0) == lax.broadcasted_iota(jnp.int32, (C, C), 1)
    eye[...] = jnp.where(square, 1.0, 0.0).astype(BF16)

    def turned(value):
        n = value.shape[1]
        return dot_nt(eye[0:n, 0:n], value).astype(BF16)

    def low(shape):
        return lax.broadcasted_iota(jnp.int32, shape, 1) < 64

    def swap(value):
        return pltpu.roll(value, 64, 1)

    def pack(left, right, odd):
        if odd:
            return jnp.where(low(left.shape), swap(left), right)
        return jnp.where(low(left.shape), left, swap(right))

    def unpack(even, odd):
        return (
            jnp.where(low(even.shape), even, swap(odd)),
            jnp.where(low(even.shape), swap(even), odd),
        )

    def both_halves(row):
        return row + swap(row)

    def over_bins(value):
        row = jnp.sum(value, axis=0, keepdims=True)
        return both_halves(row[:, :128] + row[:, 128:256] + row[:, 256:384])

    def thrice(row):
        return jnp.concatenate([row] * HJ, axis=1)

    def own_channels(ref):
        block = ref[:, pl.ds(pl.multiple_of(lax.div(p, 2) * 128, 128), 128)]
        other = swap(block)
        is_low = low(block.shape)
        even = jnp.where(is_low, block, other)
        odd = jnp.where(is_low, other, block)
        return jnp.where(x_at == 0, even, odd)

    loads["pool"].wait()
    col_parts = []
    for g in range(groups):
        loads[f"feat{g}"].wait()
        col_parts.append(dot(pool8[...], fgrp[g]))
    load("own", 5, feat_hbm.at[:, own_lanes], fext.at[pl.ds(W, PX)])
    for dy in range(3):
        for dx in range(3):
            load(f"twf{dy * 3 + dx}", 9 + dy * 3 + dx, tw_hbm.at[dy * 3 + dx, pl.ds(0, C)], twf.at[dx * 3 + 2 - dy])
            load(f"twu{dy * 3 + dx}", 18 + dy * 3 + dx, tw_hbm.at[dy * 3 + dx, pl.ds(C, C)], twu.at[dx * 3 + dy])
    load("x", 6, x_hbm, xc)
    load("xt", 7, xt_hbm, xt)
    load("spread", 8, spread_hbm, spread8)
    col_feat = jnp.concatenate(col_parts, axis=0)
    high = col_feat.astype(BF16)
    fc_hi[...] = high
    rest = (col_feat - high.astype(F32)).astype(BF16)
    loads["wb"].wait()
    rows_c = groups * J * 8
    proj2 = dot(jnp.concatenate([high, rest], axis=0), wb[...])
    proj = proj2[:rows_c] + proj2[rows_c:]
    for k in range(P // 2):
        block = proj[:, 128 * k : 128 * (k + 1)]

        def rows_of(j):
            return jnp.concatenate(
                [block[(g * J + j) * 8 : (g * J + j) * 8 + 8] for g in range(groups)], axis=0
            )

        for jj in range(HJ):
            left, right = rows_of(jj), rows_of(jj + HJ)
            for odd in range(2):
                zsend[2 * k + odd, :, 128 * jj : 128 * (jj + 1)] = pack(left, right, odd)

    pl.semaphore_wait(barrier, P - 1 + 5 * (B - 1))
    halo_down = remote(
        feat_hbm.at[pl.ds(PX - W, W), own_lanes], fext.at[pl.ds(0, W)], halo_sem, 0, "pix",
        lax.rem(p + 1, P),
    )
    halo_up = remote(
        feat_hbm.at[pl.ds(0, W), own_lanes], fext.at[pl.ds(W + PX, W)], halo_sem, 1, "pix",
        lax.rem(p + P - 1, P),
    )

    @pl.when(p < P - 1)
    def _():
        halo_down.start()

    @pl.when(p > 0)
    def _():
        halo_up.start()

    def peer_features(half):
        return remote(
            feat_hbm.at[:, pl.ds(pl.multiple_of(b * C + half * (C // 2) + (1 - x_at) * 128, 128), 128)],
            upsend.at[pl.ds(half * PX, PX)], fp_sem, half, "pix", x_peer,
        )

    fp_copies = [peer_features(0), peer_features(1)]
    def z_rows(at):
        return pl.ds(pl.multiple_of(at * R, 8), R)

    z_copies = exchange("pix", z_sem, lambda q: zsend.at[q], lambda me: zrecv.at[z_rows(me)])
    zrecv[z_rows(p), :] = zsend[p]
    pending.extend(z_copies)
    fp_copies[0].start()
    cshare = d.channels // P

    def fc_lanes(at):
        return pl.ds(pl.multiple_of(at * cshare, cshare), cshare)

    def shift_rows(source, masks, lanes_of):
        def step(r, carry):
            at = pl.multiple_of(r * W, W)
            for e in range(3):
                rows = source[pl.ds(pl.multiple_of((r + e) * W, W), W), :]
                if e != 1:
                    mask = masks[e // 2, pl.ds(r, 1), :]
                    mask = jnp.concatenate([mask] * (C // 128), axis=1)
                    rows = rows * jnp.broadcast_to(mask, rows.shape).astype(BF16)
                shifted[pl.ds(at, W), lanes_of(e)] = rows
            return carry

        lax.fori_loop(0, R, step, 0)

    def backward_lanes(e):
        return slice(e * C, (e + 1) * C)

    def forward_lanes(e):
        return backward_lanes(2 - e)

    def shift_columns(value, step):
        rows = value.shape[0]
        column = mod2(lax.broadcasted_iota(jnp.int32, value.shape, 0), W)
        if step == 1:
            return jnp.where(column == W - 1, 0.0, pltpu.roll(value, rows - 1, 0))
        return jnp.where(column == 0, 0.0, pltpu.roll(value, 1, 0))

    @pl.when(p == 0)
    def _():
        fext[pl.ds(0, W), :] = jnp.zeros((W, C), BF16)

    @pl.when(p == P - 1)
    def _():
        fext[pl.ds(W + PX, W), :] = jnp.zeros((W, C), BF16)

    @pl.when(p > 0)
    def _():
        halo_down.wait_recv()

    @pl.when(p < P - 1)
    def _():
        halo_up.wait_recv()

    loads["own"].wait()
    shift_rows(fext, mrow, forward_lanes)
    for tap in range(9):
        loads[f"twf{tap}"].wait()

    def conv_chunk(at, sign):
        rows = shifted[pl.ds(pl.multiple_of(at * OPX, W), OPX), :]
        total = None
        for dx in range(3):
            part = dot(rows, twf[3 * dx : 3 * dx + 3].reshape(3 * C, C))
            if dx != 1:
                part = shift_columns(part, sign * (dx - 1))
            total = part if total is None else total + part
        return total

    def pf_rows(at):
        return pl.ds(pl.multiple_of(at * OPX, OPX), OPX)

    def own_conv(at):
        return conv_chunk(at, 1)

    def pf_copy(step):
        return remote(pfsend.at[step], pfrecv.at[step], pf_sem, step, "br", core_peer)

    pf_copies = [pf_copy(0), pf_copy(1), remote(pfsend.at[2], pfrecv.at[2], pf_sem, 2, "br", y_peer)]
    pfsend[1] = own_conv(lax.rem(core_peer + 2, B)).astype(BF16)
    pf_copies[1].start()
    pre[...] = own_conv(y_peer)
    pf_copies[1].wait_recv()
    pfsend[2] = (pre[...] + pfrecv[1].astype(F32)).astype(BF16)
    pf_copies[2].start()

    cwp[...] = jnp.zeros_like(cwp)
    cwp[0 : d.classes, :] = cweight_t[...]
    lgp[...] = jnp.zeros_like(lgp)
    lgp[:, 0 : d.classes] = lgrad[...]
    dnorm[...] = dot(lgp[...], cwp[...])

    arrive(z_copies)
    sums = jnp.dot(hot_all[...], zrecv[...], precision=HIGH, preferred_element_type=F32)
    pooled = jnp.where(valid, sums / count, 0.0)
    centre = over_bins(pooled) / total_bins
    centred = (pooled - thrice(centre)) * valid_f
    spread = over_bins(centred * centred) / total_bins
    inv = lax.rsqrt(spread + norm_eps)
    hat = centred * thrice(inv)
    normed = hat * thrice(own_channels(bgain)) + thrice(own_channels(bshift))
    active = gelu_parts(normed)[0] * valid_f
    bhat[...] = hat
    bnorm[...] = normed
    binv[...] = jnp.broadcast_to(inv, (8, 128))
    rmsend[...] = jnp.dot(mix_all[...], active, precision=HIGH, preferred_element_type=F32).astype(BF16)

    def rm_rows(at):
        return pl.ds(pl.multiple_of(at * 8 * B, 8 * B), 8 * B)

    rm_copies = exchange("pix", rm_sem, lambda q: rmsend.at[rm_rows(q)], lambda me: rmrecv.at[rm_rows(me)])
    rmrecv[rm_rows(p), :] = rmsend[rm_rows(p), :]
    fp_copies[1].start()
    actsend[...] = active.astype(BF16)
    pending.extend(rm_copies)

    def owner_before(at):
        return lax.div(P // 2 + at, 2) <= z_at

    def to_owners(src_of, ref, sem, start=True):
        copies = []
        for at in range(4):
            target = P // 2 + at
            copy = pltpu.make_async_remote_copy(
                src_ref=src_of(at), dst_ref=ref.at[p], send_sem=sem.at[0, at],
                recv_sem=sem.at[1, p], device_id={"pix": target}, device_id_type=MESH,
            )
            copies.append(copy)

            @pl.when(p != target if start else (p != target) & owner_before(at))
            def _(copy=copy):
                copy.start()

            @pl.when(p == target)
            def _(at=at):
                ref[p] = src_of(at)[...]

        return copies

    act_copies = to_owners(lambda at: actsend, actrecv, act_sem)
    fc_copies = []
    for step in range(1, P):
        peer = lax.rem(p + step, P)
        copy = remote(fc_hi.at[:, fc_lanes(peer)], fcrecv.at[p], fc_sem, step - 1, "pix", peer)
        fc_copies.append((peer, copy))

        @pl.when(peer < p)
        def _(copy=copy):
            copy.start()

    fcrecv[p] = fc_hi[:, fc_lanes(p)]
    pending.extend(copy for _, copy in fc_copies)

    pfsend[0] = own_conv(core_peer).astype(BF16)
    pf_copies[0].start()

    arrive(rm_copies)
    for k in range(P // 2):
        even = rmrecv[64 * k : 64 * k + 32, :].astype(F32)
        odd = rmrecv[64 * k + 32 : 64 * k + 64, :].astype(F32)
        for jj in range(HJ):
            lanes = slice(128 * jj, 128 * (jj + 1))
            halves = unpack(even[:, lanes], odd[:, lanes])
            for half in range(2):
                j = jj + half * HJ
                for dy in range(3):
                    value = halves[half]
                    if dy > 0:
                        value = pltpu.roll(value, 8 * B - dy, 0)
                    if dy != 1:
                        value = value * mgrp[dy // 2]
                    for at in range(B):
                        fg[dy * lhs_rows + (at * J + j) * 8 : dy * lhs_rows + (at * J + j) * 8 + 8, 128 * k : 128 * (k + 1)] = (
                            value[8 * at : 8 * at + 8]
                        )
    for tap in range(9):
        loads[f"twu{tap}"].wait()
    block = J * 8
    per = 3 * block
    lhs = jnp.concatenate([fg[dy * lhs_rows : (dy + 1) * lhs_rows, :].astype(BF16) for dy in range(3)], axis=1)
    for dx in range(3):
        part = dot(lhs, twu[3 * dx : 3 * dx + 3].reshape(3 * C, C))
        for at in range(B):
            hsend[at * per + dx * block : at * per + (dx + 1) * block, :] = part[
                at * block : (at + 1) * block
            ].astype(BF16)

    def h_rows(at):
        return pl.ds(pl.multiple_of(at * per, per), per)

    h_copies = exchange("br", h_sem, lambda q: hsend.at[h_rows(q)], lambda me: hrecv.at[h_rows(me)])
    hrecv[h_rows(b), :] = hsend[h_rows(b), :]

    pre[...] = own_conv(b)
    pf_copies[0].wait_recv()
    pre[...] = pre[...] + pfrecv[0].astype(F32)

    def transpose_part(first, rows_of):
        def step(at, carry):
            values = rows_of(at).astype(F32)
            for dx in range(3):
                value = values if dx == 1 else shift_columns(values, dx - 1)
                fgrp[dx, first : first + half_c, pl.ds(pl.multiple_of(at * OPX, 128), OPX)] = turned(
                    value.astype(BF16)
                )
            return carry

        lax.fori_loop(0, B, step, 0)

    def my_features(at):
        rows = pl.ds(pl.multiple_of(W + at * OPX, W), OPX)
        return jnp.concatenate(
            [fext[rows, pl.ds(pl.multiple_of((x_at + 2 * z) * 128, 128), 128)] for z in range(2)], axis=1
        )

    def their_features(at):
        return jnp.concatenate(
            [upsend[pl.ds(pl.multiple_of(z * PX + at * OPX, W), OPX), :] for z in range(2)], axis=1
        )

    half_c = C // 2
    transpose_part(0, my_features)

    loads["x"].wait()
    arrive(pf_copies[2:])
    arrive(h_copies)
    pre[...] = pre[...] + pfrecv[2].astype(F32) + dot(xc[...], hrecv[...])

    def all_sum(value, send1, recv1, sem1, send2, recv2, sem2, first, second):
        send1[...] = value
        recv1[b] = value
        copies = exchange("br", sem1, lambda q: send1, lambda me: recv1.at[me])
        first()
        arrive(copies)
        pending.extend(copies)
        value = recv1[0]
        for at in range(1, B):
            value = value + recv1[at]
        send2[...] = value
        recv2[p] = value
        copies = exchange("pix", sem2, lambda q: send2, lambda me: recv2.at[me])
        second()
        arrive(copies)
        pending.extend(copies)
        value = recv2[0]
        for at in range(1, P):
            value = value + recv2[at]
        return value

    def row_sum(value):
        return jnp.sum(value, axis=0, keepdims=True)

    def tall_rows(rows):
        parts = [row[:, 128 * at : 128 * (at + 1)] for row in rows for at in range(row.shape[1] // 128)]
        parts.extend([jnp.zeros((1, 128), F32)] * (-len(parts) % 8))
        return jnp.concatenate(parts, axis=0)

    def wide_row(value, first, count):
        return jnp.concatenate([value[at : at + 1] for at in range(first, first + count)], axis=1)

    def turn_step(tap, carry):
        twf[tap] = turned(twf[tap])
        return carry

    lanes_c = C // 128
    whole = pre[...]
    stats = all_sum(
        tall_rows([row_sum(whole), row_sum(whole * whole)]),
        st1, sr1, st_sem1, st2, sr2, st_sem2,
        lambda: None, lambda: lax.fori_loop(0, 9, turn_step, 0),
    )
    total_pix = float(PX * P)
    t_mean = wide_row(stats, 0, lanes_c) / total_pix
    t_inv = lax.rsqrt(wide_row(stats, lanes_c, lanes_c) / total_pix - t_mean * t_mean + norm_eps)
    gain = tgain[...]
    shift = tshift[...]

    def norm_step(at, carry):
        rows = pl.ds(pl.multiple_of(at * W, W), W)
        hat = (pre[rows, :] - t_mean) * t_inv
        value, slope = gelu_parts(hat * gain + shift)
        hidden[rows, :] = value.astype(BF16)
        d_norm = dnorm[rows, :] * slope
        pre[rows, :] = hat
        dnorm[rows, :] = d_norm
        return carry[0] + row_sum(d_norm * hat), carry[1] + row_sum(d_norm)

    zero = jnp.zeros((1, C), F32)
    gain_sum, shift_sum = lax.fori_loop(0, Q, norm_step, (zero, zero))
    bias_sum = row_sum(lgp[...].astype(F32))
    def make_logits():
        logit = dot_nt(hidden[...], cwp[...])
        logits_out[...] = (logit[:, 0 : d.classes] + cbias[...]).astype(BF16)

    def make_class_grad():
        cwsend[...] = dot(turned(lgp[...])[0 : cwsend.shape[0]], hidden[...])
        for copy in fp_copies:
            copy.wait_recv()
        transpose_part(half_c, their_features)

    sums = all_sum(
        tall_rows([gain_sum, shift_sum, bias_sum]),
        st3, sr3, st_sem3, st4, sr4, st_sem4, make_logits, make_class_grad,
    )
    tot[...] = sums
    small_out[...] = jnp.zeros_like(small_out)
    small_out[2:3, 0 : C // B] = tot[pl.ds(b, 1), :]
    small_out[3:4, 0 : C // B] = tot[pl.ds(lanes_c + b, 1), :]
    small_out[4:5, 0:256] = wide_row(sums, 2 * lanes_c, 2)
    gain_mean = wide_row(sums, 0, lanes_c) / total_pix
    shift_mean = wide_row(sums, lanes_c, lanes_c) / total_pix

    def dp_rows(at):
        return pl.ds(pl.multiple_of(W + at * OPX, W), OPX)

    dpre = (gain * t_inv * (dnorm[...] - shift_mean - pre[...] * gain_mean)).astype(BF16)
    dpext[dp_rows(b), :] = dpre
    dp_core = remote(dpext.at[dp_rows(b)], dpext.at[dp_rows(b)], dp_sem, 0, "br", core_peer)
    dp_y = remote(dpext.at[dp_rows(b)], dpext.at[dp_rows(b)], dp_sem, 1, "br", y_peer)
    dp_on = remote(dpext.at[dp_rows(y_peer)], dpext.at[dp_rows(y_peer)], dp_sem, 2, "br", core_peer)
    dp_x = remote(dpext.at[dp_rows(b)], dpext2.at[dp_rows(b)], dp2_sem, 0, "pix", x_peer)
    pending.extend([dp_core, dp_y, dp_on, dp_x])
    dp_x.start()
    dp_core.start()
    dp_y.start()
    edge_copies = []
    for at in range(B):
        down = pltpu.make_async_remote_copy(
            src_ref=dpext.at[pl.ds(PX, W)], dst_ref=dpext.at[pl.ds(0, W)], send_sem=dphalo_sem.at[0, at],
            recv_sem=dphalo_sem.at[1, 0], device_id={"pix": lax.rem(p + 1, P), "br": at}, device_id_type=MESH,
        )
        up = pltpu.make_async_remote_copy(
            src_ref=dpext.at[pl.ds(W, W)], dst_ref=dpext.at[pl.ds(W + PX, W)], send_sem=dphalo_sem.at[0, at],
            recv_sem=dphalo_sem.at[1, 1], device_id={"pix": lax.rem(p + P - 1, P), "br": at}, device_id_type=MESH,
        )
        edge_copies.append((down, up))
    far_copies = []
    for at in range(B):
        down = pltpu.make_async_remote_copy(
            src_ref=dpext.at[pl.ds(PX, W)], dst_ref=dpext2.at[pl.ds(0, W)], send_sem=dphalo2_sem.at[0, at],
            recv_sem=dphalo2_sem.at[1, 0], device_id={"pix": lax.rem(p + 2, P), "br": at}, device_id_type=MESH,
        )
        up = pltpu.make_async_remote_copy(
            src_ref=dpext.at[pl.ds(W, W)], dst_ref=dpext2.at[pl.ds(W + PX, W)], send_sem=dphalo2_sem.at[0, at],
            recv_sem=dphalo2_sem.at[1, 0], device_id={"pix": lax.rem(p + P - 2, P), "br": at}, device_id_type=MESH,
        )
        far_copies.append((down, up))
    sends_far_down = (b == B - 1) & (x_at == 1) & (p < P - 2)
    sends_far_up = (b == 0) & (x_at == 0) & (p > 1)

    @pl.when(sends_far_down)
    def _():
        for down, up in far_copies:
            down.start()

    @pl.when(sends_far_up)
    def _():
        for down, up in far_copies:
            up.start()


    @pl.when((b == B - 1) & (p < P - 1))
    def _():
        for down, up in edge_copies:
            down.start()

    @pl.when((b == 0) & (p > 0))
    def _():
        for down, up in edge_copies:
            up.start()

    @pl.when(p == 0)
    def _():
        dpext[pl.ds(0, W), :] = jnp.zeros((W, C), BF16)

    @pl.when(p == P - 1)
    def _():
        dpext[pl.ds(W + PX, W), :] = jnp.zeros((W, C), BF16)


    for peer, copy in fc_copies:

        @pl.when(peer > p)
        def _(copy=copy):
            copy.start()

    def half_block(at, half):
        return pl.ds(pl.multiple_of(W + at * OPX + half * (OPX // 2), 32), OPX // 2)

    dp2_core = remote(dpext2.at[dp_rows(b)], dpext2.at[dp_rows(b)], dp2_sem, 1, "br", core_peer)
    dp2_x = remote(dpext.at[half_block(y_peer, 0)], dpext2.at[half_block(y_peer, 0)], dp2_sem, 2, "pix", x_peer)
    dp2_y = remote(dpext2.at[half_block(b, 1)], dpext2.at[half_block(b, 1)], dp2_sem, 3, "br", y_peer)
    dp2_on = [
        remote(dpext2.at[half_block(y_peer, n)], dpext2.at[half_block(y_peer, n)], dp2_sem, 4 + n, "br", core_peer)
        for n in range(2)
    ]
    pending.extend([dp2_core, dp2_x, dp2_y] + dp2_on)
    dp_x.wait_recv()
    dp2_y.start()
    dp2_core.start()
    dp_y.wait_recv()
    dp2_x.start()
    dp_on.start()

    cq = C // B

    def cq_lanes(at):
        return pl.ds(pl.multiple_of(at * cq, cq), cq)

    cw_copies1 = exchange(
        "br", cw_sem1, lambda q: cwsend.at[:, cq_lanes(q)], lambda me: cwr1.at[me]
    )
    cwr1[b] = cwsend[:, cq_lanes(b)]
    pending.extend(cw_copies1)

    dp_core.wait_recv()
    dp_on.wait_recv()

    @pl.when(p > 0)
    def _():
        edge_copies[0][0].wait_recv()

    @pl.when(p < P - 1)
    def _():
        edge_copies[0][1].wait_recv()

    loads["xt"].wait()
    own_columns = xt[h_rows(b), :]
    for at in range(B):
        drecv[at * per : (at + 1) * per, :] = dot(own_columns, dpext[W + at * OPX : W + (at + 1) * OPX, :]).astype(BF16)
    cols = []
    for dx in range(3):
        cols.append(
            jnp.concatenate(
                [drecv[at * per + dx * block : at * per + (dx + 1) * block, :] for at in range(B)], axis=0
            )
        )
    parts = []
    for dy in range(3):
        part = dot_nt(cols[0], twu[dy]) + dot_nt(cols[1], twu[3 + dy]) + dot_nt(cols[2], twu[6 + dy])
        if dy != 1:
            mask = jnp.concatenate(
                [mgrp[dy // 2, 8 * at : 8 * at + 8, :] for at in range(B) for j in range(J)], axis=0
            )
            part = part * jnp.concatenate([mask] * (C // 128), axis=1)
        if dy > 0:
            part = pltpu.roll(part, dy, 0)
        parts.append(part)
    d_mix = parts[0] + parts[1] + parts[2]

    def group_rows(value, j):
        return jnp.concatenate(
            [value[(at * J + j) * 8 : (at * J + j) * 8 + 8] for at in range(B)], axis=0
        )

    for k in range(P // 2):
        value = d_mix[:, 128 * k : 128 * (k + 1)]
        for jj in range(HJ):
            left, right = group_rows(value, jj), group_rows(value, jj + HJ)
            for odd in range(2):
                at = 32 * (2 * k + odd)
                drsend[at : at + 32, 128 * jj : 128 * (jj + 1)] = pack(left, right, odd).astype(BF16)
    dr_copies = exchange("pix", dr_sem, lambda q: drsend.at[rm_rows(q)], lambda me: drrecv.at[rm_rows(me)])
    drrecv[rm_rows(p), :] = drsend[rm_rows(p), :]
    pending.extend(dr_copies)

    def o_lanes(at):
        return pl.ds(at * 128, 128)

    def from_all(ref, sem, sources):
        for src in sources:

            @pl.when(p != src)
            def _(src=src):
                pltpu.make_async_remote_copy(
                    src_ref=ref.at[0], dst_ref=ref.at[src], send_sem=sem.at[0, 0],
                    recv_sem=sem.at[1, src], device_id={"pix": p}, device_id_type=MESH,
                ).wait_recv()

    dw_copies = to_owners(lambda at: drecv.at[:, o_lanes(at)], dwrecv, dw_sem, start=False)

    shift_rows(dpext, mrow, backward_lanes)
    half_rows = C // 4

    def tap_product(tap, first):
        dy, dx = lax.div(tap, 3), lax.rem(tap, 3)
        return dot(fgrp[dx, first : first + half_c, 0:PX], shifted[:, pl.ds(pl.multiple_of((2 - dy) * C, C), C)])

    def own_step(tap, carry):
        keep[tap] = tap_product(tap, 0)
        return carry

    lax.fori_loop(0, 5, own_step, 0)
    dp2_x.wait_recv()
    dp2_on[0].start()
    dp2_y.wait_recv()
    dp2_on[1].start()
    lax.fori_loop(5, 9, own_step, 0)

    arrive(cw_copies1)
    cw2[...] = cwr1[0] + cwr1[1] + cwr1[2] + cwr1[3]
    c_part = cwsend.shape[0] // P

    def cw_rows(at):
        return pl.ds(pl.multiple_of(at * c_part, 8), c_part)

    cw_copies2 = exchange("pix", cw_sem2, lambda q: cw2.at[cw_rows(q)], lambda me: cwr2.at[me])
    cwr2[p] = cw2[cw_rows(p), :]
    pending.extend(cw_copies2)

    arrive(dr_copies)
    d_active = jnp.dot(mix_t[...], drrecv[...].astype(F32), precision=HIGH, preferred_element_type=F32)
    hat = bhat[...]
    d_normed = d_active * valid_f * gelu_parts(bnorm[...])[1]
    gain_part = over_bins(d_normed * hat)
    shift_part = over_bins(d_normed)
    scale = thrice(own_channels(bgain) * binv[0:1])
    d_pooled = scale * (d_normed - thrice(shift_part / total_bins) - hat * thrice(gain_part / total_bins)) * valid_f
    dssend[...] = (d_pooled / count).astype(BF16)
    dsrecv[p] = dssend[...]
    ds_copies = []
    for step in range(1, P // 2):
        copy = remote(dssend, dsrecv.at[p], ds_sem, step - 1, "pix", lax.rem(p + 2 * step, P))
        copy.start()
        ds_copies.append(copy)
    ds_across = []
    for step in range(P // 2):
        at = lax.rem(p + P - 2 * step, P)
        ds_across.append(remote(dsrecv.at[at], dsrecv.at[at], ds_sem, P // 2 - 1 + step, "pix", x_peer))
    ds_across[0].start()
    small = jnp.concatenate([gain_part, shift_part, jnp.zeros((6, 128), F32)], axis=0)
    smsend[...] = small
    sm_copies = exchange("pix", sm_sem, lambda q: smsend, lambda me: smrecv.at[me])
    smrecv[p] = small
    pending.extend(ds_copies + ds_across + sm_copies)

    for at in range(4):

        @pl.when((p != P // 2 + at) & jnp.logical_not(owner_before(at)))
        def _(at=at):
            dw_copies[at].start()

    @pl.when(x_at == 0)
    def _():
        dpext2[pl.ds(0, W), :] = dpext[pl.ds(PX, W), :]

    @pl.when(x_at == 1)
    def _():
        dpext2[pl.ds(W + PX, W), :] = dpext[pl.ds(W, W), :]

    @pl.when(p == 1)
    def _():
        dpext2[pl.ds(0, W), :] = jnp.zeros((W, C), BF16)

    @pl.when(p == P - 2)
    def _():
        dpext2[pl.ds(W + PX, W), :] = jnp.zeros((W, C), BF16)

    @pl.when((x_at == 1) & (p > 1))
    def _():
        far_copies[0][0].wait_recv()

    @pl.when((x_at == 0) & (p < P - 2))
    def _():
        far_copies[0][1].wait_recv()

    dp2_core.wait_recv()
    arrive(dp2_on)
    shift_rows(dpext2, mrow2, backward_lanes)

    def half_of(half):
        return pl.ds(half * half_rows, half_rows)

    def z_copy(tap, half):
        rows = half_of(half)
        return remote(
            sendx.at[tap, rows], recvz.at[tap, rows], zz_sem, tap * 2 + half, "pix", lax.rem(p + P - 2, P)
        )

    def a_rows(tap):
        return pl.ds(pl.multiple_of(lax.rem(tap, 3) * half_rows, 128), half_rows)

    def a_copy(tap):
        rows = pl.ds(pl.multiple_of((1 - z_at) * half_rows, 128), half_rows)
        return remote(sendx.at[tap, rows], pfrecv.at[lax.div(tap, 3), a_rows(tap)], a_sem, tap, "pix", lax.rem(p + 2 - 4 * z_at + 2 * P, P))

    def twg_copy(tap):
        return pltpu.make_async_copy(recvz.at[tap, half_of(0)], twg_hbm.at[tap], twg_sem.at[tap])

    def finish(tap):
        a_copy(tap).wait_recv()
        rows = pl.ds(pl.multiple_of(z_at * half_rows, 128), half_rows)
        recvz[tap, 0:half_rows, :] = (
            keep[tap, rows, :] + pfrecv[lax.div(tap, 3), a_rows(tap), :].astype(F32)
        ).astype(BF16)

    def peer_step(tap, carry):
        keep[tap] = keep[tap] + tap_product(tap, half_c)

        @pl.when((z_at == 0) | (z_at == 3))
        def _():
            sendx[tap] = keep[tap].astype(BF16)

        @pl.when(z_at == 3)
        def _():
            z_copy(tap, 0).start()
            z_copy(tap, 1).start()

        @pl.when(z_at == 0)
        def _():
            a_copy(tap).start()

        return carry

    lax.fori_loop(0, 9, peer_step, 0)

    def chain_step(tap, carry):
        @pl.when((z_at == 1) | (z_at == 2))
        def _():
            for half in range(2):
                z_copy(tap, half).wait_recv()
                rows = half_of(half)
                keep[tap, rows, :] = keep[tap, rows, :] + recvz[tap, rows, :].astype(F32)
                if half == 0:
                    sendx[tap, rows, :] = keep[tap, rows, :].astype(BF16)

                    @pl.when(z_at == 2)
                    def _():
                        z_copy(tap, 0).start()

                    @pl.when(z_at == 1)
                    def _():
                        a_copy(tap).start()

                else:

                    @pl.when(z_at == 2)
                    def _():
                        sendx[tap, rows, :] = keep[tap, rows, :].astype(BF16)
                        z_copy(tap, 1).start()

        return carry

    def chain_to(tap):
        lax.fori_loop(tap, tap + 1, chain_step, 0)

    chain_to(0)
    for step in range(1, P // 2):
        ds_copies[step - 1].wait_recv()
        ds_across[step].start()


    def unpack_all(source, target):
        for k in range(P // 2):
            even = source[2 * k].astype(F32)
            odd = source[2 * k + 1].astype(F32)
            for jj in range(HJ):
                lanes = slice(128 * jj, 128 * (jj + 1))
                halves = unpack(even[:, lanes], odd[:, lanes])
                for half in range(2):
                    j = jj + half * HJ
                    target[j * NB : (j + 1) * NB, 128 * k : 128 * (k + 1)] = halves[half].astype(BF16)

    arrive(cw_copies2)
    value = cwr2[0]
    for at in range(1, P):
        value = value + cwr2[at]
    cw3[...] = value
    cw_copies3 = exchange("pix", cw_sem3, lambda q: cw3, lambda me: cwr3.at[cw_rows(me)])
    cwr3[cw_rows(p), :] = value
    pending.extend(cw_copies3)

    chain_to(1)
    arrive(ds_across)
    unpack_all(dsrecv, ds_all)
    hot_mine = hot_own[...].astype(BF16)
    d_col = [dot(hot_mine, ds_all[j * NB : (j + 1) * NB, :]) for j in range(J)]
    d_col = jnp.concatenate(
        [d_col[j][8 * g : 8 * g + 8] for g in range(groups) for j in range(J)], axis=0
    ).astype(BF16)
    esend[...] = dot_nt(d_col, wb[...]).astype(BF16)

    def e_lanes(at):
        return pl.ds(pl.multiple_of(at * C, C), C)

    e_copies = exchange("br", e_sem, lambda q: esend.at[:, e_lanes(q)], lambda me: erecv.at[me])
    erecv[b] = esend[:, e_lanes(b)]
    pending.extend(e_copies)

    chain_to(2)
    shift_rows(dpext, mrow, backward_lanes)
    def back_step(at, carry):
        fg[pf_rows(at), :] = conv_chunk(at, -1)
        return carry

    lax.fori_loop(0, B // 2, back_step, 0)
    chain_to(3)
    lax.fori_loop(B // 2, B, back_step, 0)
    chain_to(4)
    for copy in pf_copies + h_copies:
        copy.wait_send()
    up_copies = []
    up_rows = 9 * 128
    for at in range(4):
        target = P // 2 + at
        up_copies.append(
            pltpu.make_async_remote_copy(
                src_ref=upsend.at[pl.ds(at * up_rows, up_rows)], dst_ref=uprecv.at[lax.rem(p, P // 2)], send_sem=up_sem.at[0, at],
                recv_sem=up_sem.at[1, p], device_id={"pix": target}, device_id_type=MESH,
            )
        )

    @pl.when(z_at >= 2)
    def _():
        from_all(actrecv, act_sem, range(P))
        unpack_all(actrecv, hsend)
        from_all(dwrecv, dw_sem, range(P))
        k_rows = P * B * block
        for dx in range(3):
            value = jnp.concatenate(
                [
                    dwrecv[at, per * owner + block * dx : per * owner + block * (dx + 1), :]
                    for at in range(P)
                    for owner in range(B)
                ],
                axis=0,
            )
            value = turned(value)
            for part in range(k_rows // C):
                pfsend[part, 128 * dx : 128 * (dx + 1), :] = value[:, C * part : C * (part + 1)]
        t_grp, k_grp = halo_rows((8 * B * P, 1), 0, 0)
        here_grp = jnp.where(k_grp < Q, row_info(t_grp)[0], -3)

        def up_step(dy, carry):
            mix = row_mix(t_grp + (dy - 1), g_row, i_row, here_grp)
            mix_high = mix.astype(BF16)
            mix_low = (mix - mix_high.astype(F32)).astype(BF16)
            for pair in range(J // 2):
                two = []
                for j in (2 * pair, 2 * pair + 1):
                    act = hsend[j * NB : (j + 1) * NB, :]
                    two.append(dot(mix_high, act) + dot(mix_low, act))
                for at in range(P * B):
                    value = jnp.concatenate([rows[8 * at : 8 * at + 8] for rows in two], axis=0)
                    to = at * block + 16 * pair
                    fgrp[to // C, to % C : to % C + 16, 0:C] = value.astype(BF16)
            total = None
            for part in range(k_rows // C):
                term = dot(pfsend[part], fgrp[part, 0:C, 0:C])
                total = term if total is None else total + term
            for at in range(4):
                upsend[pl.ds(pl.multiple_of(at * up_rows + dy * 384, 128), 384), :] = total[
                    :, 128 * at : 128 * (at + 1)
                ].astype(BF16)
            return carry

        lax.fori_loop(0, 3, up_step, 0)
        for at, copy in enumerate(up_copies):

            @pl.when(p != P // 2 + at)
            def _(copy=copy):
                copy.start()

            @pl.when(p == P // 2 + at)
            def _(at=at):
                uprecv[at] = upsend[at * up_rows : (at + 1) * up_rows, :]

    chain_to(5)
    arrive([copy for _, copy in fc_copies])
    hot16 = hot_all[...].astype(BF16)

    def eight(at, row):
        pair = fcrecv[at, row // 16 * 16 : row // 16 * 16 + 16, :].astype(F32)
        return pair[row % 16 : row % 16 + 8]

    for j in range(J):
        rows = jnp.concatenate(
            [eight(at, (g * J + j) * 8) for at in range(P) for g in range(groups)],
            axis=0,
        )
        fp_all[j * NB : (j + 1) * NB, :] = dot(hot16, rows.astype(BF16)).astype(BF16)
    fp_t[...] = turned(fp_all[...])

    bwg_out[...] = dot(fp_t[...], ds_all[...])
    arrive(sm_copies)
    for k in range(P // 2):
        lanes = slice(128 * k, 128 * (k + 1))
        is_low = low((1, 128))
        small_out[0:1, lanes] = jnp.where(is_low, smrecv[2 * k, 0:1, :], smrecv[2 * k + 1, 0:1, :])
        small_out[1:2, lanes] = jnp.where(is_low, smrecv[2 * k, 1:2, :], smrecv[2 * k + 1, 1:2, :])

    chain_to(6)
    arrive(e_copies)
    loads["spread"].wait()
    for g in range(groups):
        rows = jnp.concatenate([erecv[at, block * g : block * (g + 1), :] for at in range(B)], axis=0)
        total = fg[gpx * g : gpx * (g + 1), :] + dot(spread8[...], rows)
        shifted[gpx * g : gpx * (g + 1), 0:C] = total.astype(BF16)
    fg_copy = pltpu.make_async_copy(shifted.at[:, pl.ds(0, C)], fg_hbm, out_sem.at[0])
    fg_copy.start()

    chain_to(7)

    @pl.when(z_at < 2)
    def _():
        def most(tap, carry):
            finish(tap)
            twg_copy(tap).start()
            return carry

        lax.fori_loop(0, 7, most, 0)

    chain_to(8)

    @pl.when(z_at < 2)
    def _():
        def last(tap, carry):
            finish(tap)
            twg_copy(tap).start()
            return carry

        lax.fori_loop(7, 9, last, 0)

    @pl.when(z_at >= 2)
    def _():
        for src in range(4):

            @pl.when(p != P // 2 + src)
            def _(src=src):
                pltpu.make_async_remote_copy(
                    src_ref=upsend.at[pl.ds(0, up_rows)], dst_ref=uprecv.at[src], send_sem=up_sem.at[0, 0],
                    recv_sem=up_sem.at[1, P // 2 + src], device_id={"pix": p}, device_id_type=MESH,
                ).wait_recv()

        def gather(tap, carry):
            rows = pl.ds(pl.multiple_of(tap * 128, 128), 128)
            value = jnp.concatenate([uprecv[at, rows, :] for at in range(4)], axis=0)
            recvz[tap, 0:half_rows, :] = turned(value)
            twg_copy(tap).start()
            return carry

        lax.fori_loop(0, 9, gather, 0)

    arrive(cw_copies3)
    cwg_out[...] = cwr3[0 : d.classes, :]

    pending.extend(fp_copies)

    for copy in pending:
        copy.wait_send()

    @pl.when(p < P - 1)
    def _():
        halo_down.wait_send()

    @pl.when(p > 0)
    def _():
        halo_up.wait_send()

    @pl.when((b == B - 1) & (p < P - 1))
    def _():
        for down, up in edge_copies:
            down.wait_send()

    @pl.when((b == 0) & (p > 0))
    def _():
        for down, up in edge_copies:
            up.wait_send()

    @pl.when(sends_far_down)
    def _():
        for down, up in far_copies:
            down.wait_send()

    @pl.when(sends_far_up)
    def _():
        for down, up in far_copies:
            up.wait_send()

    for at in range(4):

        @pl.when(p != P // 2 + at)
        def _(at=at):
            dw_copies[at].wait_send()
            act_copies[at].wait_send()

        @pl.when((z_at >= 2) & (p != P // 2 + at))
        def _(at=at):
            up_copies[at].wait_send()

    def sent(tap, carry):
        @pl.when(z_at >= 2)
        def _():
            z_copy(tap, 0).wait_send()
            z_copy(tap, 1).wait_send()

        @pl.when(z_at < 2)
        def _():
            a_copy(tap).wait_send()

        return carry

    lax.fori_loop(0, 9, sent, 0)
    fg_copy.wait()

    def handed(tap, carry):
        twg_copy(tap).wait()
        return carry

    lax.fori_loop(0, 9, handed, 0)


def spread_tables(width, own, rows):
    side = max(bin_sides)
    count = len(bin_sides)
    cols = shifted_columns(bin_sides, width, side)
    up = np.zeros((own, width, count, 3, side, 8), np.float32)
    for m in range(own):
        up[m, :, :, :, :, m] = cols.transpose(2, 0, 1, 3)
    up = up.reshape(own * width, count * 3 * side * 8)
    bins = column_bins(bin_sides, width, side)
    pool = np.zeros((count, side, 8, 8, width), np.float32)
    spread = np.zeros((8, width, count, side, 8), np.float32)
    for r in range(8):
        pool[:, :, r, r, :] = bins
        spread[r, :, :, :, r] = bins.transpose(2, 0, 1)
    bf16 = jnp.bfloat16
    return (
        jnp.asarray(up, bf16),
        jnp.asarray(up.T, bf16),
        jnp.asarray(pool.reshape(count, side * 8, 8 * width), bf16),
        jnp.asarray(spread.reshape(8 * width, count * side * 8), bf16),
    )


def on_device_fused(
    features,
    branch_weight,
    branch_gain,
    branch_shift,
    trunk_weight,
    trunk_gain,
    trunk_shift,
    class_weight,
    class_bias,
    heights,
    logit_grad,
):
    P, B = lax.axis_size("pix"), lax.axis_size("br")
    d = Shape(features, branch_weight, class_weight, heights, P, B)
    W, C, J, NB, R, PX, OPX = d.width, d.ch, d.side, d.bins, d.rows, d.px, d.own_px
    CH, K = d.channels, d.classes
    per = 3 * J * 8
    groups = R // 8
    up, up_t, pool, spread = spread_tables(W, d.own, R)
    half = C // 4
    kp = -(-K // (8 * P)) * 8 * P
    vmem, sem = pltpu.VMEM, pltpu.SemaphoreType.DMA
    scratch = dict(
        fext=vmem((PX + 2 * W, C), BF16), shifted=vmem((PX, 3 * C), BF16), fgrp=vmem((groups, 8 * W, CH), BF16),
        wb=vmem((CH, C), BF16), twf=vmem((9, C, C), BF16), twu=vmem((9, C, C), BF16),
        xc=vmem(up.shape, BF16), xt=vmem(up_t.shape, BF16), pool8=vmem(pool.shape[1:], BF16), spread8=vmem(spread.shape, BF16),
        fc_hi=vmem((groups * J * 8, CH), BF16), zsend=vmem((P, R, 384), F32), zrecv=vmem((P * R, 384), F32),
        fcrecv=vmem((P, groups * J * 8, CH // P), BF16), pfsend=vmem((B - 1, OPX, C), BF16), pfrecv=vmem((B - 1, OPX, C), BF16),
        hidden=vmem((OPX, C), BF16),
        hot_all=vmem((NB, P * R), F32), mix_all=vmem((8 * B * P, NB), F32), mix_t=vmem((NB, 8 * B * P), F32), hot_own=vmem((R, NB), F32),
        mrow=vmem((2, 32, 128), F32), mrow2=vmem((2, 32, 128), F32), mgrp=vmem((2, 8 * B, 128), F32),
        bhat=vmem((NB, 384), F32), bnorm=vmem((NB, 384), F32), binv=vmem((8, 128), F32),
        rmsend=vmem((8 * B * P, 384), BF16), rmrecv=vmem((8 * B * P, 384), BF16), actsend=vmem((NB, 384), BF16), actrecv=vmem((P, NB, 384), BF16),
        hsend=vmem((B * per, C), BF16), hrecv=vmem((B * per, C), BF16),
        st1=vmem((8, 128), F32), st2=vmem((8, 128), F32), st3=vmem((16, 128), F32), st4=vmem((16, 128), F32),
        sr1=vmem((B, 8, 128), F32), sr2=vmem((P, 8, 128), F32), sr3=vmem((B, 16, 128), F32), sr4=vmem((P, 16, 128), F32), tot=vmem((16, 128), F32),
        cwp=vmem((256, C), BF16), lgp=vmem((OPX, 256), BF16), cwsend=vmem((kp, C), F32), cwr1=vmem((B, kp, C // B), F32),
        cw2=vmem((kp, C // B), F32), cwr2=vmem((P, kp // P, C // B), F32), cw3=vmem((kp // P, C // B), F32), cwr3=vmem((kp, C // B), F32),
        dpext=vmem((PX + 2 * W, C), BF16), dpext2=vmem((PX + 2 * W, C), BF16), drecv=vmem((B * per, C), BF16),
        drsend=vmem((8 * B * P, 384), BF16), drrecv=vmem((8 * B * P, 384), BF16),
        dwrecv=vmem((P, B * per, 128), BF16),
        dssend=vmem((NB, 384), BF16), dsrecv=vmem((P, NB, 384), BF16), smsend=vmem((8, 128), F32), smrecv=vmem((P, 8, 128), F32),
        ds_all=vmem((J * NB, C), BF16), fp_all=vmem((J * NB, CH // P), BF16), fp_t=vmem((CH // P, J * NB), BF16), esend=vmem((groups * J * 8, CH), BF16),
        erecv=vmem((B, groups * J * 8, C), BF16), fg=vmem((PX, C), F32), keep=vmem((9, 2 * half, C), F32),
        sendx=vmem((9, 2 * half, C), BF16),
        recvz=vmem((9, 2 * half, C), BF16),
        upsend=vmem((4 * 9 * 128, 128), BF16), uprecv=vmem((4, 9 * 128, 128), BF16), eye=vmem((C, C), BF16),
        load_sem=sem((27,)), out_sem=sem((2,)), twg_sem=sem((9,)), halo_sem=sem((2, 2)), z_sem=sem((2, P)), fc_sem=sem((2, P)), pf_sem=sem((2, B)),
        rm_sem=sem((2, P)), act_sem=sem((2, P)), h_sem=sem((2, B)),
        st_sem1=sem((2, B)), st_sem2=sem((2, P)), st_sem3=sem((2, B)), st_sem4=sem((2, P)),
        cw_sem1=sem((2, B)), cw_sem2=sem((2, P)), cw_sem3=sem((2, P)),
        dp_sem=sem((2, B)), dphalo_sem=sem((2, B)), dp2_sem=sem((2, 6)), dphalo2_sem=sem((2, B)), fp_sem=sem((2, 2)), dr_sem=sem((2, P)), dw_sem=sem((2, P)), ds_sem=sem((2, P)),
        sm_sem=sem((2, P)), e_sem=sem((2, B)), zz_sem=sem((2, 24)), a_sem=sem((2, 9)), up_sem=sem((2, P)),
    )
    hbm = pl.BlockSpec(memory_space=pl.ANY)
    local = pl.BlockSpec(memory_space=pltpu.VMEM)
    scalars = pl.BlockSpec(memory_space=pltpu.SMEM)

    def out(shape, dtype):
        return jax.ShapeDtypeStruct(shape, dtype)

    outs = pl.pallas_call(
        functools.partial(fused_kernel, d),
        out_shape=(
            out((OPX, K), BF16), out((PX, C), BF16), out((CH // P, C), F32), out((9, half, C), BF16),
            out((K, C // B), F32), out((8, C), F32),
        ),
        in_specs=[hbm] * 7 + [local] * 7 + [scalars],
        out_specs=(local, hbm, local, hbm, local, local),
        scratch_shapes=list(scratch.values()),
        compiler_params=pltpu.CompilerParams(
            collective_id=0, has_side_effects=True, vmem_limit_bytes=127 * 512 * 1024
        ),
    )(
        features.reshape(PX, CH), branch_weight[0], trunk_weight.reshape(9, 2 * C, C), up, up_t, pool, spread,
        branch_gain, branch_shift, trunk_gain[None], trunk_shift[None], class_weight.T, class_bias[None],
        logit_grad.reshape(OPX, K), heights,
    )

    def hand_on(*refs):
        src, small, dst, smalls = refs[:5], refs[5], refs[6:11], refs[11:16]
        held, wide, sems = refs[16:21], {1: refs[21], 3: refs[22]}, refs[23]
        parts = []
        for at in (1, 3, 0, 2, 4):
            rows = src[at].shape[0]
            cuts = {1: 8, 3: 9}.get(at, 1)
            for cut in range(cuts):
                part = pl.ds(cut * (rows // cuts), rows // cuts)
                n = len(parts)
                parts.append(
                    (
                        at,
                        part,
                        pltpu.make_async_copy(src[at].at[part], held[at].at[part], sems.at[0, n]),
                        pltpu.make_async_copy(wide.get(at, held[at]).at[part], dst[at].at[part], sems.at[1, n]),
                    )
                )
        for _, _, there, _ in parts:
            there.start()
        for at, ref in enumerate(smalls):
            ref[...] = small[at : at + 1, 0 : ref.shape[1]]
        for at, part, there, back in parts:
            there.wait()
            if at in wide:
                wide[at][part] = held[at][part].astype(F32)
            back.start()
        for _, _, _, back in parts:
            back.wait()

    logits, fg, bwg, twg, cwg, bgg, bsg, tgg, tsg, cbg = pl.pallas_call(
        hand_on,
        out_shape=tuple(out(o.shape, BF16 if at == 0 else F32) for at, o in enumerate(outs[:5]))
        + tuple(out((1, n), F32) for n in (C, C, C // B, C // B, K)),
        in_specs=[hbm] * 5 + [local],
        out_specs=tuple([hbm] * 5 + [local] * 5),
        scratch_shapes=[vmem(o.shape, o.dtype) for o in outs[:5]]
        + [vmem(outs[1].shape, F32), vmem(outs[3].shape, F32), sem((2, 24))],
        compiler_params=pltpu.CompilerParams(vmem_limit_bytes=127 * 512 * 1024),
    )(*outs)
    return (
        logits.reshape(d.own, W, K), fg.reshape(R, W, C), bwg[None], bgg, bsg,
        twg.reshape(1, 3, 3, half, C), tgg[0], tsg[0], cwg.T, cbg[0],
    )


def solution(mesh):
    in_specs = (
        P("pix", None, None),
        P("br", None, None),
        P("br", None),
        P("br", None),
        P("br", None, None, None, None),
        P(),
        P(),
        P(),
        P(),
        P(),
        P(("pix", "br"), None, None),
    )
    out_specs = (
        P(("pix", "br"), None, None),
        P("pix", None, "br"),
        P("br", "pix", None),
        P("br", None),
        P("br", None),
        P("br", None, None, "pix", None),
        P("br"),
        P("br"),
        P("br", None),
        P(),
    )
    fused = mesh.shape["pix"] == 8 and mesh.shape["br"] == 4
    return jax.shard_map(
        on_device_fused if fused else on_device, mesh=mesh, in_specs=in_specs, out_specs=out_specs, check_vma=False
    )
```

```python
import functools

import jax
import jax.numpy as jnp
import numpy as np
from jax import lax
from jax.experimental import pallas as pl
from jax.experimental.pallas import tpu as pltpu
from jax.sharding import PartitionSpec as P

bin_sides = (1, 2, 3, 6)
norm_eps = 1e-05


def padded_2(cells, sides, width):
    for axis, dim in sides:
        count = lax.axis_size(axis)
        ends = count - 1
        head = lax.slice_in_dim(cells, 0, width, axis=dim)
        tail = lax.slice_in_dim(cells, cells.shape[dim] - width, cells.shape[dim], axis=dim)
        cells = jnp.concatenate(
            [
                lax.ppermute(tail, axis, [(i, (i + 1) % count) for i in range(ends)]),
                cells,
                lax.ppermute(head, axis, [((i + 1) % count, i) for i in range(ends)]),
            ],
            axis=dim,
        )
    return cells


def activate(value):
    return jax.nn.gelu(value, approximate=True)


def gelu_slope(value):
    unused, pull = jax.vjp(activate, value)
    return pull(jnp.ones_like(value))[0]


def image_of(starts, row_ids):
    return jnp.sum((starts[None, :] <= row_ids[:, None]).astype(jnp.int32), axis=1) - 1


def exact_dot(left, right):
    return jnp.dot(left, right, precision=lax.Precision.HIGHEST, preferred_element_type=jnp.float32)


def contract(left, right, left_dim, right_dim):
    return lax.dot_general(
        left, right, (((left_dim,), (right_dim,)), ((), ())), preferred_element_type=jnp.float32
    )


def row_columns(sides, width, most_side):
    out = np.zeros((len(sides), width, most_side), np.float32)
    for b, side in enumerate(sides):
        for x in range(width):
            numer = (2 * x + 1) * side - width
            first = numer // (2 * width) if numer >= 0 else 0
            frac = (numer - 2 * width * first) / (2.0 * width) if numer >= 0 else 0.0
            second = min(first + 1, side - 1)
            out[b, x, first] += 1.0 - frac
            out[b, x, second] += frac
    return out


def shifted_columns(sides, width, most_side):
    cols = row_columns(sides, width, most_side)
    out = np.zeros((len(sides), 3, width, most_side), np.float32)
    for at, step in enumerate((-1, 0, 1)):
        for x in range(width):
            if 0 <= x + step < width:
                out[:, at, x] = cols[:, x + step]
    return out


def column_bins(sides, width, most_side):
    out = np.zeros((len(sides), most_side, width), np.float32)
    for b, side in enumerate(sides):
        for j in range(side):
            out[b, j, j * width // side : ((j + 1) * width + side - 1) // side] = 1.0
    return out


def split_dot(left, right, **kw):
    high = left.astype(jnp.bfloat16)
    low = (left - high.astype(jnp.float32)).astype(jnp.bfloat16)
    return jnp.dot(high, right, preferred_element_type=jnp.float32) + jnp.dot(
        low, right, preferred_element_type=jnp.float32
    )


def on_device(
    features,
    branch_weight,
    branch_gain,
    branch_shift,
    trunk_weight,
    trunk_gain,
    trunk_shift,
    class_weight,
    class_bias,
    heights,
    logit_grad,
):
    rows_dev, width, channels = features.shape
    branch_ch = branch_weight.shape[2]
    classes = class_weight.shape[1]
    images = heights.shape[0]
    most_side = max(bin_sides)
    pix_count = lax.axis_size("pix")
    br_count = lax.axis_size("br")
    pix_at = lax.axis_index("pix")
    br_at = lax.axis_index("br")
    own_rows = rows_dev // br_count
    total_pix = float(rows_dev * width * pix_count)
    slice_width = channels // br_count
    bf16 = jnp.bfloat16
    side = jnp.sum(jnp.where(jnp.arange(len(bin_sides)) == br_at, jnp.array(bin_sides, jnp.int32), 0))
    starts = jnp.cumsum(heights) - heights
    bin_ids = jnp.arange(most_side, dtype=jnp.int32)
    in_use = bin_ids < side
    ext_ids = pix_at * rows_dev - 1 + jnp.arange(rows_dev + 2, dtype=jnp.int32)
    on_canvas = (ext_ids >= 0) & (ext_ids < rows_dev * pix_count)
    ext_image = jnp.where(on_canvas, image_of(starts, ext_ids), -1)
    owner = ext_image[:, None] == jnp.arange(images, dtype=jnp.int32)[None, :]
    height = jnp.maximum(jnp.sum(jnp.where(owner, heights[None, :], 0), axis=1), 1)
    place = ext_ids - jnp.sum(jnp.where(owner, starts[None, :], 0), axis=1)
    lower = bin_ids[None, :] * height[:, None] // side
    upper = ((bin_ids[None, :] + 1) * height[:, None] + side - 1) // side
    member = in_use[None, :] & (place[:, None] >= lower) & (place[:, None] < upper)
    row_hot = (
        (owner.T[:, None, :] & member.T[None, :, :])
        .reshape(images * most_side, rows_dev + 2)[:, 1:-1]
        .astype(jnp.float32)
    )
    numer = (2 * place + 1) * side - height
    ahead = numer >= 0
    first = jnp.where(ahead, numer // (2 * height), 0)
    frac = jnp.where(
        ahead,
        (numer - 2 * height * first).astype(jnp.float32) / (2 * height).astype(jnp.float32),
        0.0,
    )
    second = jnp.minimum(first + 1, side - 1)
    mix = (bin_ids[:, None] == first[None, :]).astype(jnp.float32) * (1.0 - frac)[None, :]
    mix = mix + (bin_ids[:, None] == second[None, :]).astype(jnp.float32) * frac[None, :]
    interp = (owner.T.astype(jnp.float32)[:, None, :] * mix[None]).reshape(
        images * most_side, rows_dev + 2
    )
    image_low = bin_ids[None, :] * heights[:, None] // side
    image_up = ((bin_ids[None, :] + 1) * heights[:, None] + side - 1) // side
    col_low = bin_ids * width // side
    col_up = ((bin_ids + 1) * width + side - 1) // side
    valid = in_use[:, None] & in_use[None, :]
    counts = jnp.where(
        valid[None], (image_up - image_low)[:, :, None] * (col_up - col_low)[None, None, :], 1
    ).astype(jnp.float32)
    valid_f = valid.astype(jnp.float32)[None, :, :, None]
    all_cols = jnp.asarray(shifted_columns(bin_sides, width, most_side))
    all_bins = jnp.asarray(column_bins(bin_sides, width, most_side), bf16)
    own_bins = lax.dynamic_index_in_dim(all_bins, br_at, 0, False)

    col_feat = jnp.einsum("jx,rxc->jrc", own_bins, features, preferred_element_type=jnp.float32)
    col_proj = split_dot(col_feat.reshape(-1, channels), branch_weight[0])
    col_proj = col_proj.reshape(most_side, rows_dev, branch_ch)
    pool_part = jnp.einsum("nr,jrc->njc", row_hot, col_proj, precision=lax.Precision.HIGHEST)
    sums = lax.psum(pool_part, "pix").reshape(images, most_side, most_side, branch_ch)
    pooled = sums / counts[..., None]
    total_bins = (images * side * side).astype(jnp.float32)
    centre = jnp.sum(pooled * valid_f, axis=(0, 1, 2)) / total_bins
    centred = (pooled - centre) * valid_f
    b_inv = lax.rsqrt(jnp.sum(centred * centred, axis=(0, 1, 2)) / total_bins + norm_eps)
    b_hat = centred * b_inv
    normed = b_hat * branch_gain[0] + branch_shift[0]
    active = (activate(normed) * valid_f).reshape(images * most_side, most_side, branch_ch)
    row_mix = jnp.einsum("nr,njc->rjc", interp, active, precision=lax.Precision.HIGHEST).astype(bf16)

    def keep(step):
        return (ext_image[1 + step : 1 + step + rows_dev] == ext_image[1:-1]).astype(bf16)

    own_slice = lax.dynamic_slice_in_dim(features, br_at * slice_width, slice_width, 2)
    feat_ext = padded_2(own_slice, (("pix", 0),), 1)
    feat_pad = jnp.pad(feat_ext, ((0, 0), (1, 1), (0, 0)))
    feat_weight = trunk_weight[0, :, :, :slice_width]
    up_weight = trunk_weight[0, :, :, slice_width:]
    feat_sum = jnp.zeros((rows_dev * width, branch_ch), jnp.float32)
    up_sum = [jnp.zeros((rows_dev * most_side, branch_ch), jnp.float32) for _ in range(3)]
    for at in range(3):
        band = feat_pad[at : at + rows_dev] * keep(at - 1)[:, None, None]
        up_band = (row_mix[at : at + rows_dev] * keep(at - 1)[:, None, None]).reshape(-1, branch_ch)
        for to in range(3):
            window = band[:, to : to + width].reshape(-1, slice_width)
            feat_sum = feat_sum + jnp.dot(
                window, feat_weight[at, to], preferred_element_type=jnp.float32
            )
            up_sum[to] = up_sum[to] + jnp.dot(
                up_band, up_weight[at, to], preferred_element_type=jnp.float32
            )
    pre = lax.psum_scatter(
        feat_sum.astype(bf16).reshape(rows_dev, width, branch_ch), "br", scatter_dimension=0, tiled=True
    ).astype(jnp.float32)
    up_all = jnp.stack(up_sum).reshape(3, br_count, own_rows, most_side, branch_ch).astype(bf16)
    up_all = lax.all_to_all(up_all, "br", 1, 0, tiled=False)
    pre = pre + jnp.einsum(
        "btxj,btrjc->rxc", all_cols.astype(bf16), up_all, preferred_element_type=jnp.float32
    )

    both = ("pix", "br")
    first_sum, square_sum = lax.psum((jnp.sum(pre, (0, 1)), jnp.sum(pre * pre, (0, 1))), both)
    t_mean = first_sum / total_pix
    t_inv = lax.rsqrt(square_sum / total_pix - t_mean * t_mean + norm_eps)
    t_hat = (pre - t_mean) * t_inv
    t_norm = t_hat * trunk_gain + trunk_shift
    hidden = activate(t_norm).astype(bf16).reshape(-1, branch_ch)
    logits = jnp.dot(hidden, class_weight, preferred_element_type=jnp.float32) + class_bias
    logits = logits.reshape(own_rows, width, classes).astype(bf16)
    grad_flat = logit_grad.reshape(-1, classes)
    weight_part = contract(hidden, grad_flat, 0, 0)
    bias_part = jnp.sum(grad_flat.astype(jnp.float32), axis=0)
    d_norm = contract(grad_flat, class_weight, 1, 1).reshape(pre.shape) * gelu_slope(t_norm)
    gain_part, shift_part, bias_part = lax.psum(
        (jnp.sum(d_norm * t_hat, (0, 1)), jnp.sum(d_norm, (0, 1)), bias_part), both
    )
    weight_part = lax.psum(lax.psum_scatter(weight_part, "br", scatter_dimension=0, tiled=True), "pix")
    d_pre = (
        trunk_gain * t_inv * (d_norm - shift_part / total_pix - t_hat * gain_part / total_pix)
    ).astype(bf16)

    d_cols = jnp.einsum(
        "btxj,rxc->btrjc", all_cols.astype(bf16), d_pre, preferred_element_type=jnp.float32
    ).astype(bf16)
    d_cols = lax.all_to_all(d_cols, "br", 0, 2, tiled=True)[0]
    d_mix = jnp.zeros((rows_dev + 2, most_side, branch_ch), jnp.float32)
    up_taps = []
    for at in range(3):
        part = jnp.zeros((rows_dev * most_side, branch_ch), jnp.float32)
        kept = d_cols * keep(at - 1)[None, :, None, None]
        up_band = row_mix[at : at + rows_dev].reshape(-1, branch_ch)
        for to in range(3):
            part = part + contract(kept[to].reshape(-1, branch_ch), up_weight[at, to], 1, 1)
            up_taps.append(contract(up_band, kept[to].reshape(-1, branch_ch), 0, 0))
        d_mix = d_mix.at[at : at + rows_dev].add(part.reshape(rows_dev, most_side, branch_ch))
    d_bin_part = jnp.einsum("nr,rjc->njc", interp, d_mix, precision=lax.Precision.HIGHEST)
    d_active = lax.psum(d_bin_part, "pix").reshape(images, most_side, most_side, branch_ch)
    d_normed = d_active * valid_f * gelu_slope(normed)
    branch_gain_part = jnp.sum(d_normed * b_hat, axis=(0, 1, 2))
    branch_shift_part = jnp.sum(d_normed, axis=(0, 1, 2))
    d_pooled = (
        branch_gain[0]
        * b_inv
        * (d_normed - branch_shift_part / total_bins - b_hat * branch_gain_part / total_bins)
        * valid_f
    )
    d_sums = (d_pooled / counts[..., None]).reshape(images * most_side, most_side, branch_ch)

    d_all = lax.all_gather(d_pre, "br", axis=0, tiled=True)
    d_pad = jnp.pad(padded_2(d_all, (("pix", 0),), 1), ((0, 0), (1, 1), (0, 0)))
    d_flat = d_all.reshape(-1, branch_ch)
    d_own = jnp.zeros((rows_dev * width, slice_width), jnp.float32)
    feat_taps = []
    for at in range(3):
        band = feat_pad[at : at + rows_dev] * keep(at - 1)[:, None, None]
        back = d_pad[2 - at : 2 - at + rows_dev] * keep(1 - at)[:, None, None]
        for to in range(3):
            window = band[:, to : to + width].reshape(-1, slice_width)
            feat_taps.append(contract(window, d_flat, 0, 0))
            source = back[:, 2 - to : 2 - to + width].reshape(-1, branch_ch)
            d_own = d_own + contract(source, feat_weight[at, to], 1, 1)
    taps = jnp.concatenate([jnp.stack(feat_taps), jnp.stack(up_taps)], axis=1).astype(bf16)
    trunk_weight_grad = lax.psum_scatter(taps, "pix", scatter_dimension=1, tiled=True)
    trunk_weight_grad = trunk_weight_grad.astype(jnp.float32).reshape(1, 3, 3, -1, branch_ch)

    d_col = jnp.einsum("nr,njc->jrc", row_hot, d_sums, precision=lax.Precision.HIGHEST).astype(bf16)
    spread = contract(d_col.reshape(-1, branch_ch), branch_weight[0], 1, 1).astype(bf16)
    spread = spread.reshape(1, most_side, rows_dev, br_count, slice_width)
    spread = lax.all_to_all(spread, "br", 3, 0, tiled=False)[:, 0]
    feature_grad = jnp.einsum(
        "bjx,bjrc->rxc", all_bins, spread, preferred_element_type=jnp.float32
    ) + d_own.reshape(rows_dev, width, slice_width)
    branch_term = contract(col_feat.astype(bf16).reshape(-1, channels), d_col.reshape(-1, branch_ch), 0, 0)
    branch_weight_grad = lax.psum_scatter(branch_term, "pix", scatter_dimension=0, tiled=True)[None]
    start = br_at * (branch_ch // br_count)
    return (
        logits,
        feature_grad,
        branch_weight_grad,
        branch_gain_part[None],
        branch_shift_part[None],
        trunk_weight_grad,
        lax.dynamic_slice_in_dim(gain_part, start, branch_ch // br_count, 0),
        lax.dynamic_slice_in_dim(shift_part, start, branch_ch // br_count, 0),
        weight_part,
        bias_part,
    )


MESH = pl.DeviceIdType.MESH
HIGH = lax.Precision.HIGHEST
F32 = jnp.float32
BF16 = jnp.bfloat16


def mod2(value, by):
    return lax.bitwise_and(value, jnp.full_like(value, by - 1))


def div2(value, by):
    return lax.shift_right_logical(value, jnp.full_like(value, by.bit_length() - 1))


def dot(left, right):
    return jnp.dot(left, right, preferred_element_type=F32)


def dot_nt(left, right):
    return lax.dot_general(left, right, (((1,), (1,)), ((), ())), preferred_element_type=F32)


def dot_tn(left, right):
    return lax.dot_general(left, right, (((0,), (0,)), ((), ())), preferred_element_type=F32)


def gelu_parts(value):
    inner = 0.7978845608 * (value + 0.044715 * value * value * value)
    tanh = jnp.tanh(inner)
    half = 0.5 * (1.0 + tanh)
    slope = half + 0.5 * value * (1.0 - tanh * tanh) * (
        0.7978845608 * (1.0 + 0.134145 * value * value)
    )
    return value * half, slope


class Shape:
    def __init__(self, features, branch_weight, class_weight, heights, pix, br):
        self.rows, self.width, self.channels = features.shape
        self.ch = branch_weight.shape[2]
        self.classes = class_weight.shape[1]
        self.images = heights.shape[0]
        self.pix, self.br = pix, br
        self.side = max(bin_sides)
        self.bins = self.side * self.images
        self.own = self.rows // br
        self.px = self.rows * self.width
        self.own_px = self.own * self.width
        self.all_rows = self.rows * pix


def fused_kernel(
    d,
    feat_hbm, bw_hbm, tw_hbm, x_hbm, xt_hbm, pool_hbm, spread_hbm,
    bgain, bshift, tgain, tshift, cweight_t, cbias, lgrad, heights,
    logits_out, fg_hbm, bwg_out, twg_hbm, cwg_out, small_out,
    fext, shifted, fgrp, wb, twf, twu, xc, xt, pool8, spread8,
    fc_hi, zsend, zrecv, fcrecv, pfsend, pfrecv, hidden,
    hot_all, mix_all, mix_t, hot_own, mrow, mrow2, mgrp,
    bhat, bnorm, binv, rmsend, rmrecv, actsend, actrecv, hsend, hrecv,
    st1, st2, st3, st4, sr1, sr2, sr3, sr4, tot,
    cwp, lgp, cwsend, cwr1, cw2, cwr2, cw3, cwr3,
    dpext, dpext2, drecv, drsend, drrecv, dwrecv, dssend, dsrecv, smsend, smrecv, ds_all,
    fp_all, fp_t, esend, erecv, fg, keep, sendx, recvz, upsend, uprecv, eye,
    load_sem, out_sem, twg_sem, halo_sem, z_sem, fc_sem, pf_sem, rm_sem, act_sem, h_sem,
    st_sem1, st_sem2, st_sem3, st_sem4, cw_sem1, cw_sem2, cw_sem3,
    dp_sem, dphalo_sem, dp2_sem, dphalo2_sem, fp_sem, dr_sem, dw_sem, ds_sem, sm_sem, e_sem, zz_sem, a_sem, up_sem,
):
    W, C, J, NB, P, B = d.width, d.ch, d.side, d.bins, d.pix, d.br
    PX, OPX, R, Q = d.px, d.own_px, d.rows, d.own
    HJ = J // 2
    lhs_rows = 8 * B * J
    pre = fg.at[pl.ds(3 * lhs_rows, OPX)]
    dnorm = fg.at[pl.ds(3 * lhs_rows + OPX, OPX)]
    p = lax.axis_index("pix")
    b = lax.axis_index("br")
    x_at = lax.rem(p, 2)
    z_at = lax.div(p, 2)
    x_peer = p + 1 - 2 * x_at
    core_peer = b + 1 - 2 * lax.rem(b, 2)
    y_peer = lax.rem(b + 2, B)
    side = jnp.where(b == 0, 1, jnp.where(b == 1, 2, jnp.where(b == 2, 3, 6)))
    side_f = side.astype(F32)

    def remote(src, dst, sem, at, axis, peer):
        return pltpu.make_async_remote_copy(
            src_ref=src, dst_ref=dst, send_sem=sem.at[0, at], recv_sem=sem.at[1, at],
            device_id={axis: peer}, device_id_type=MESH,
        )

    def exchange(axis, sem, src_of, dst_of):
        count, me = (P, p) if axis == "pix" else (B, b)
        copies = []
        for step in range(1, count):
            peer = lax.rem(me + step, count)
            copy = remote(src_of(peer), dst_of(me), sem, step - 1, axis, peer)
            copy.start()
            copies.append(copy)
        return copies

    def arrive(copies):
        for copy in copies:
            copy.wait_recv()

    pending = []

    own_lanes = pl.ds(pl.multiple_of(b * C, C), C)
    groups = R // 8
    gpx = 8 * W
    loads = {}

    def load(name, at, src, dst):
        loads[name] = pltpu.make_async_copy(src, dst, load_sem.at[at])
        loads[name].start()

    load("pool", 0, pool_hbm.at[b], pool8)
    for g in range(groups):
        load(f"feat{g}", 1 + g, feat_hbm.at[pl.ds(g * gpx, gpx)], fgrp.at[g])
    load("wb", 4, bw_hbm, wb)

    barrier = pltpu.get_barrier_semaphore()
    for step in range(1, P):
        pl.semaphore_signal(barrier, inc=1, device_id={"pix": lax.rem(p + step, P)}, device_id_type=MESH)
    for step in range(1, B):
        pl.semaphore_signal(barrier, inc=1, device_id={"br": lax.rem(b + step, B)}, device_id_type=MESH)

    for step in range(1, B):
        for to in (p + 1, p + P - 1, p + 2, p + P - 2):
            pl.semaphore_signal(
                barrier, inc=1, device_id={"pix": lax.rem(to, P), "br": lax.rem(b + step, B)},
                device_id_type=MESH,
            )

    tall = [heights[g] for g in range(d.images)]
    starts = [jnp.int32(0)]
    for g in range(d.images - 1):
        starts.append(starts[-1] + tall[g])

    def row_info(t):
        image = jnp.full(t.shape, -1, jnp.int32)
        height = jnp.ones(t.shape, jnp.int32)
        start = jnp.zeros(t.shape, jnp.int32)
        for g in range(d.images):
            reached = t >= starts[g]
            image = jnp.where(reached, g, image)
            height = jnp.where(reached, tall[g], height)
            start = jnp.where(reached, starts[g], start)
        image = jnp.where(t >= d.all_rows, -2, image)
        return image, height.astype(F32), (t - start).astype(F32)

    def bin_index(shape, axis):
        n = lax.broadcasted_iota(jnp.int32, shape, axis)
        return mod2(n, d.images), div2(n, d.images)

    def floor_div(a, by):
        return jnp.floor((a + 0.5) / by)

    def row_hot(t, g, i):
        image, height, place = row_info(t)
        i_f = i.astype(F32)
        lower = floor_div(i_f * height, side_f)
        upper = floor_div((i_f + 1.0) * height + (side_f - 1.0), side_f)
        inside = (image == g) & (i < side) & (place >= lower) & (place < upper)
        return jnp.where(inside, 1.0, 0.0)

    def row_mix(t, g, i, image_at=None):
        image, height, place = row_info(t)
        twice = 2.0 * height
        numer = (2.0 * place + 1.0) * side_f - height
        first = jnp.where(numer >= 0.0, floor_div(numer, twice), 0.0)
        frac = jnp.where(numer >= 0.0, (numer - twice * first) / twice, 0.0)
        second = jnp.minimum(first + 1.0, side_f - 1.0)
        i_f = i.astype(F32)
        value = jnp.where(i_f == first, 1.0 - frac, 0.0) + jnp.where(i_f == second, frac, 0.0)
        value = jnp.where(image == g, value, 0.0)
        if image_at is not None:
            value = jnp.where(image == image_at, value, 0.0)
        return value

    def halo_rows(shape, axis, first):
        n = lax.broadcasted_iota(jnp.int32, shape, axis)
        k, owner, dev = mod2(n, 8), mod2(div2(n, 8), B), div2(n, 8 * B)
        return first + dev * R + owner * Q + k, k

    g_col, i_col = bin_index((NB, 1), 0)
    g_row, i_row = bin_index((1, NB), 1)
    t_row = lax.broadcasted_iota(jnp.int32, (1, d.all_rows), 1)
    hot_all[...] = row_hot(t_row, g_col, i_col)
    t_own = lax.broadcasted_iota(jnp.int32, (R, 1), 0) + p * R
    hot_own[...] = row_hot(t_own, g_row, i_row)
    t_halo, _ = halo_rows((8 * B * P, 1), 0, -1)
    mix_all[...] = row_mix(t_halo, g_row, i_row)
    t_halo, _ = halo_rows((1, 8 * B * P), 1, -1)
    mix_t[...] = row_mix(t_halo, g_col, i_col)
    t_own = lax.broadcasted_iota(jnp.int32, (32, 128), 0) + p * R
    here = row_info(t_own)[0]
    t_peer = lax.broadcasted_iota(jnp.int32, (32, 128), 0) + x_peer * R
    here_peer = row_info(t_peer)[0]
    t_grp, k_grp = halo_rows((8 * B, 128), 0, p * R)
    here_grp = row_info(t_grp)[0]
    for at, step in enumerate((-1, 1)):
        mrow2[at] = jnp.where(row_info(t_peer + step)[0] == here_peer, 1.0, 0.0)
        mrow[at] = jnp.where(row_info(t_own + step)[0] == here, 1.0, 0.0)
        mgrp[at] = jnp.where((row_info(t_grp + step)[0] == here_grp) & (k_grp < Q), 1.0, 0.0)

    tall_col = jnp.ones((NB, 1), F32)
    for g in range(d.images):
        tall_col = jnp.where(g_col == g, tall[g].astype(F32), tall_col)
    i_f = i_col.astype(F32)
    row_count = floor_div((i_f + 1.0) * tall_col + (side_f - 1.0), side_f) - floor_div(
        i_f * tall_col, side_f
    )
    lane = lax.broadcasted_iota(jnp.int32, (1, HJ * 128), 1)
    j_lane = div2(lane, 128) + jnp.where(mod2(lane, 128) >= 64, HJ, 0)
    j_f = j_lane.astype(F32)
    col_count = floor_div((j_f + 1.0) * W + (side_f - 1.0), side_f) - floor_div(j_f * W, side_f)
    valid = (i_col < side) & (j_lane < side)
    valid_f = jnp.where(valid, 1.0, 0.0)
    count = jnp.where(valid, row_count * col_count, 1.0)
    total_bins = side_f * side_f * float(d.images)

    square = lax.broadcasted_iota(jnp.int32, (C, C), 0) == lax.broadcasted_iota(jnp.int32, (C, C), 1)
    eye[...] = jnp.where(square, 1.0, 0.0).astype(BF16)

    def turned(value):
        n = value.shape[1]
        return dot_nt(eye[0:n, 0:n], value).astype(BF16)

    def low(shape):
        return lax.broadcasted_iota(jnp.int32, shape, 1) < 64

    def swap(value):
        return pltpu.roll(value, 64, 1)

    def pack(left, right, odd):
        if odd:
            return jnp.where(low(left.shape), swap(left), right)
        return jnp.where(low(left.shape), left, swap(right))

    def unpack(even, odd):
        return (
            jnp.where(low(even.shape), even, swap(odd)),
            jnp.where(low(even.shape), swap(even), odd),
        )

    def both_halves(row):
        return row + swap(row)

    def over_bins(value):
        row = jnp.sum(value, axis=0, keepdims=True)
        return both_halves(row[:, :128] + row[:, 128:256] + row[:, 256:384])

    def thrice(row):
        return jnp.concatenate([row] * HJ, axis=1)

    def own_channels(ref):
        block = ref[:, pl.ds(pl.multiple_of(lax.div(p, 2) * 128, 128), 128)]
        other = swap(block)
        is_low = low(block.shape)
        even = jnp.where(is_low, block, other)
        odd = jnp.where(is_low, other, block)
        return jnp.where(x_at == 0, even, odd)

    loads["pool"].wait()
    col_parts = []
    for g in range(groups):
        loads[f"feat{g}"].wait()
        col_parts.append(dot(pool8[...], fgrp[g]))
    load("own", 5, feat_hbm.at[:, own_lanes], fext.at[pl.ds(W, PX)])
    for dy in range(3):
        for dx in range(3):
            load(f"twf{dy * 3 + dx}", 9 + dy * 3 + dx, tw_hbm.at[dy * 3 + dx, pl.ds(0, C)], twf.at[dx * 3 + 2 - dy])
            load(f"twu{dy * 3 + dx}", 18 + dy * 3 + dx, tw_hbm.at[dy * 3 + dx, pl.ds(C, C)], twu.at[dx * 3 + dy])
    load("x", 6, x_hbm, xc)
    load("xt", 7, xt_hbm, xt)
    load("spread", 8, spread_hbm, spread8)
    col_feat = jnp.concatenate(col_parts, axis=0)
    high = col_feat.astype(BF16)
    fc_hi[...] = high
    rest = (col_feat - high.astype(F32)).astype(BF16)
    loads["wb"].wait()
    rows_c = groups * J * 8
    proj2 = dot(jnp.concatenate([high, rest], axis=0), wb[...])
    proj = proj2[:rows_c] + proj2[rows_c:]
    for k in range(P // 2):
        block = proj[:, 128 * k : 128 * (k + 1)]

        def rows_of(j):
            return jnp.concatenate(
                [block[(g * J + j) * 8 : (g * J + j) * 8 + 8] for g in range(groups)], axis=0
            )

        for jj in range(HJ):
            left, right = rows_of(jj), rows_of(jj + HJ)
            for odd in range(2):
                zsend[2 * k + odd, :, 128 * jj : 128 * (jj + 1)] = pack(left, right, odd)

    pl.semaphore_wait(barrier, P - 1 + 5 * (B - 1))
    halo_down = remote(
        feat_hbm.at[pl.ds(PX - W, W), own_lanes], fext.at[pl.ds(0, W)], halo_sem, 0, "pix",
        lax.rem(p + 1, P),
    )
    halo_up = remote(
        feat_hbm.at[pl.ds(0, W), own_lanes], fext.at[pl.ds(W + PX, W)], halo_sem, 1, "pix",
        lax.rem(p + P - 1, P),
    )

    @pl.when(p < P - 1)
    def _():
        halo_down.start()

    @pl.when(p > 0)
    def _():
        halo_up.start()

    def peer_features(half):
        return remote(
            feat_hbm.at[:, pl.ds(pl.multiple_of(b * C + half * (C // 2) + (1 - x_at) * 128, 128), 128)],
            upsend.at[pl.ds(half * PX, PX)], fp_sem, half, "pix", x_peer,
        )

    fp_copies = [peer_features(0), peer_features(1)]
    def z_rows(at):
        return pl.ds(pl.multiple_of(at * R, 8), R)

    z_copies = exchange("pix", z_sem, lambda q: zsend.at[q], lambda me: zrecv.at[z_rows(me)])
    zrecv[z_rows(p), :] = zsend[p]
    pending.extend(z_copies)
    fp_copies[0].start()
    cshare = d.channels // P

    def fc_lanes(at):
        return pl.ds(pl.multiple_of(at * cshare, cshare), cshare)

    def shift_rows(source, masks, lanes_of):
        def step(r, carry):
            at = pl.multiple_of(r * W, W)
            for e in range(3):
                rows = source[pl.ds(pl.multiple_of((r + e) * W, W), W), :]
                if e != 1:
                    mask = masks[e // 2, pl.ds(r, 1), :]
                    mask = jnp.concatenate([mask] * (C // 128), axis=1)
                    rows = rows * jnp.broadcast_to(mask, rows.shape).astype(BF16)
                shifted[pl.ds(at, W), lanes_of(e)] = rows
            return carry

        lax.fori_loop(0, R, step, 0)

    def backward_lanes(e):
        return slice(e * C, (e + 1) * C)

    def forward_lanes(e):
        return backward_lanes(2 - e)

    def shift_columns(value, step):
        rows = value.shape[0]
        column = mod2(lax.broadcasted_iota(jnp.int32, value.shape, 0), W)
        if step == 1:
            return jnp.where(column == W - 1, 0.0, pltpu.roll(value, rows - 1, 0))
        return jnp.where(column == 0, 0.0, pltpu.roll(value, 1, 0))

    @pl.when(p == 0)
    def _():
        fext[pl.ds(0, W), :] = jnp.zeros((W, C), BF16)

    @pl.when(p == P - 1)
    def _():
        fext[pl.ds(W + PX, W), :] = jnp.zeros((W, C), BF16)

    @pl.when(p > 0)
    def _():
        halo_down.wait_recv()

    @pl.when(p < P - 1)
    def _():
        halo_up.wait_recv()

    loads["own"].wait()
    shift_rows(fext, mrow, forward_lanes)
    for tap in range(9):
        loads[f"twf{tap}"].wait()

    def conv_chunk(at, sign):
        rows = shifted[pl.ds(pl.multiple_of(at * OPX, W), OPX), :]
        total = None
        for dx in range(3):
            part = dot(rows, twf[3 * dx : 3 * dx + 3].reshape(3 * C, C))
            if dx != 1:
                part = shift_columns(part, sign * (dx - 1))
            total = part if total is None else total + part
        return total

    def pf_rows(at):
        return pl.ds(pl.multiple_of(at * OPX, OPX), OPX)

    def own_conv(at):
        return conv_chunk(at, 1)

    def pf_copy(step):
        return remote(pfsend.at[step], pfrecv.at[step], pf_sem, step, "br", core_peer)

    pf_copies = [pf_copy(0), pf_copy(1), remote(pfsend.at[2], pfrecv.at[2], pf_sem, 2, "br", y_peer)]
    pfsend[1] = own_conv(lax.rem(core_peer + 2, B)).astype(BF16)
    pf_copies[1].start()
    pre[...] = own_conv(y_peer)
    pf_copies[1].wait_recv()
    pfsend[2] = (pre[...] + pfrecv[1].astype(F32)).astype(BF16)
    pf_copies[2].start()

    cwp[...] = jnp.zeros_like(cwp)
    cwp[0 : d.classes, :] = cweight_t[...]
    lgp[...] = jnp.zeros_like(lgp)
    lgp[:, 0 : d.classes] = lgrad[...]
    dnorm[...] = dot(lgp[...], cwp[...])

    arrive(z_copies)
    sums = jnp.dot(hot_all[...], zrecv[...], precision=HIGH, preferred_element_type=F32)
    pooled = jnp.where(valid, sums / count, 0.0)
    centre = over_bins(pooled) / total_bins
    centred = (pooled - thrice(centre)) * valid_f
    spread = over_bins(centred * centred) / total_bins
    inv = lax.rsqrt(spread + norm_eps)
    hat = centred * thrice(inv)
    normed = hat * thrice(own_channels(bgain)) + thrice(own_channels(bshift))
    active = gelu_parts(normed)[0] * valid_f
    bhat[...] = hat
    bnorm[...] = normed
    binv[...] = jnp.broadcast_to(inv, (8, 128))
    rmsend[...] = jnp.dot(mix_all[...], active, precision=HIGH, preferred_element_type=F32).astype(BF16)

    def rm_rows(at):
        return pl.ds(pl.multiple_of(at * 8 * B, 8 * B), 8 * B)

    rm_copies = exchange("pix", rm_sem, lambda q: rmsend.at[rm_rows(q)], lambda me: rmrecv.at[rm_rows(me)])
    rmrecv[rm_rows(p), :] = rmsend[rm_rows(p), :]
    fp_copies[1].start()
    actsend[...] = active.astype(BF16)
    pending.extend(rm_copies)

    def owner_before(at):
        return lax.div(P // 2 + at, 2) <= z_at

    def in_column_order(copies, wanted=None):
        for column in range(2):
            for at, copy in enumerate(copies):
                go = (p != P // 2 + at) & (lax.rem(x_at + column, 2) == at % 2)
                if wanted is not None:
                    go = go & wanted(at)

                @pl.when(go)
                def _(copy=copy):
                    copy.start()

    def to_owners(src_of, ref, sem, only_before=False):
        copies = []
        for at in range(4):
            target = P // 2 + at
            copy = pltpu.make_async_remote_copy(
                src_ref=src_of(at), dst_ref=ref.at[p], send_sem=sem.at[0, at],
                recv_sem=sem.at[1, p], device_id={"pix": target}, device_id_type=MESH,
            )
            copies.append(copy)

            @pl.when(p == target)
            def _(at=at):
                ref[p] = src_of(at)[...]

        in_column_order(copies, owner_before if only_before else None)
        return copies

    act_copies = to_owners(lambda at: actsend, actrecv, act_sem)
    fc_copies = []
    for step in range(1, P):
        peer = lax.rem(p + step, P)
        copy = remote(fc_hi.at[:, fc_lanes(peer)], fcrecv.at[p], fc_sem, step - 1, "pix", peer)
        fc_copies.append((peer, copy))

        @pl.when(peer < p)
        def _(copy=copy):
            copy.start()

    fcrecv[p] = fc_hi[:, fc_lanes(p)]
    pending.extend(copy for _, copy in fc_copies)

    pfsend[0] = own_conv(core_peer).astype(BF16)
    pf_copies[0].start()

    arrive(rm_copies)
    for k in range(P // 2):
        even = rmrecv[64 * k : 64 * k + 32, :].astype(F32)
        odd = rmrecv[64 * k + 32 : 64 * k + 64, :].astype(F32)
        for jj in range(HJ):
            lanes = slice(128 * jj, 128 * (jj + 1))
            halves = unpack(even[:, lanes], odd[:, lanes])
            for half in range(2):
                j = jj + half * HJ
                for dy in range(3):
                    value = halves[half]
                    if dy > 0:
                        value = pltpu.roll(value, 8 * B - dy, 0)
                    if dy != 1:
                        value = value * mgrp[dy // 2]
                    for at in range(B):
                        fg[dy * lhs_rows + (at * J + j) * 8 : dy * lhs_rows + (at * J + j) * 8 + 8, 128 * k : 128 * (k + 1)] = (
                            value[8 * at : 8 * at + 8]
                        )
    for tap in range(9):
        loads[f"twu{tap}"].wait()
    block = J * 8
    per = 3 * block
    lhs = jnp.concatenate([fg[dy * lhs_rows : (dy + 1) * lhs_rows, :].astype(BF16) for dy in range(3)], axis=1)
    for dx in range(3):
        part = dot(lhs, twu[3 * dx : 3 * dx + 3].reshape(3 * C, C))
        for at in range(B):
            hsend[at * per + dx * block : at * per + (dx + 1) * block, :] = part[
                at * block : (at + 1) * block
            ].astype(BF16)

    def h_rows(at):
        return pl.ds(pl.multiple_of(at * per, per), per)

    h_copies = exchange("br", h_sem, lambda q: hsend.at[h_rows(q)], lambda me: hrecv.at[h_rows(me)])
    hrecv[h_rows(b), :] = hsend[h_rows(b), :]

    pre[...] = own_conv(b)
    pf_copies[0].wait_recv()
    pre[...] = pre[...] + pfrecv[0].astype(F32)

    def transpose_part(first, rows_of):
        def step(at, carry):
            values = rows_of(at).astype(F32)
            for dx in range(3):
                value = values if dx == 1 else shift_columns(values, dx - 1)
                fgrp[dx, first : first + half_c, pl.ds(pl.multiple_of(at * OPX, 128), OPX)] = turned(
                    value.astype(BF16)
                )
            return carry

        lax.fori_loop(0, B, step, 0)

    def my_features(at):
        rows = pl.ds(pl.multiple_of(W + at * OPX, W), OPX)
        return jnp.concatenate(
            [fext[rows, pl.ds(pl.multiple_of((x_at + 2 * z) * 128, 128), 128)] for z in range(2)], axis=1
        )

    def their_features(at):
        return jnp.concatenate(
            [upsend[pl.ds(pl.multiple_of(z * PX + at * OPX, W), OPX), :] for z in range(2)], axis=1
        )

    half_c = C // 2
    transpose_part(0, my_features)

    loads["x"].wait()
    arrive(pf_copies[2:])
    arrive(h_copies)
    pre[...] = pre[...] + pfrecv[2].astype(F32) + dot(xc[...], hrecv[...])

    def all_sum(value, send1, recv1, sem1, send2, recv2, sem2, first, second):
        send1[...] = value
        recv1[b] = value
        copies = exchange("br", sem1, lambda q: send1, lambda me: recv1.at[me])
        first()
        arrive(copies)
        pending.extend(copies)
        value = recv1[0]
        for at in range(1, B):
            value = value + recv1[at]
        send2[...] = value
        recv2[p] = value
        copies = exchange("pix", sem2, lambda q: send2, lambda me: recv2.at[me])
        second()
        arrive(copies)
        pending.extend(copies)
        value = recv2[0]
        for at in range(1, P):
            value = value + recv2[at]
        return value

    def row_sum(value):
        return jnp.sum(value, axis=0, keepdims=True)

    def tall_rows(rows):
        parts = [row[:, 128 * at : 128 * (at + 1)] for row in rows for at in range(row.shape[1] // 128)]
        parts.extend([jnp.zeros((1, 128), F32)] * (-len(parts) % 8))
        return jnp.concatenate(parts, axis=0)

    def wide_row(value, first, count):
        return jnp.concatenate([value[at : at + 1] for at in range(first, first + count)], axis=1)

    def turn_step(tap, carry):
        twf[tap] = turned(twf[tap])
        return carry

    lanes_c = C // 128
    whole = pre[...]
    stats = all_sum(
        tall_rows([row_sum(whole), row_sum(whole * whole)]),
        st1, sr1, st_sem1, st2, sr2, st_sem2,
        lambda: None, lambda: lax.fori_loop(0, 9, turn_step, 0),
    )
    total_pix = float(PX * P)
    t_mean = wide_row(stats, 0, lanes_c) / total_pix
    t_inv = lax.rsqrt(wide_row(stats, lanes_c, lanes_c) / total_pix - t_mean * t_mean + norm_eps)
    gain = tgain[...]
    shift = tshift[...]

    def norm_step(at, carry):
        rows = pl.ds(pl.multiple_of(at * W, W), W)
        hat = (pre[rows, :] - t_mean) * t_inv
        value, slope = gelu_parts(hat * gain + shift)
        hidden[rows, :] = value.astype(BF16)
        d_norm = dnorm[rows, :] * slope
        pre[rows, :] = hat
        dnorm[rows, :] = d_norm
        return carry[0] + row_sum(d_norm * hat), carry[1] + row_sum(d_norm)

    zero = jnp.zeros((1, C), F32)
    gain_sum, shift_sum = lax.fori_loop(0, Q, norm_step, (zero, zero))
    bias_sum = row_sum(lgp[...].astype(F32))
    def make_logits():
        logit = dot_nt(hidden[...], cwp[...])
        logits_out[...] = (logit[:, 0 : d.classes] + cbias[...]).astype(BF16)

    def make_class_grad():
        cwsend[...] = dot(turned(lgp[...])[0 : cwsend.shape[0]], hidden[...])
        for copy in fp_copies:
            copy.wait_recv()
        transpose_part(half_c, their_features)

    sums = all_sum(
        tall_rows([gain_sum, shift_sum, bias_sum]),
        st3, sr3, st_sem3, st4, sr4, st_sem4, make_logits, make_class_grad,
    )
    tot[...] = sums
    small_out[...] = jnp.zeros_like(small_out)
    small_out[2:3, 0 : C // B] = tot[pl.ds(b, 1), :]
    small_out[3:4, 0 : C // B] = tot[pl.ds(lanes_c + b, 1), :]
    small_out[4:5, 0:256] = wide_row(sums, 2 * lanes_c, 2)
    gain_mean = wide_row(sums, 0, lanes_c) / total_pix
    shift_mean = wide_row(sums, lanes_c, lanes_c) / total_pix

    def dp_rows(at):
        return pl.ds(pl.multiple_of(W + at * OPX, W), OPX)

    dpre = (gain * t_inv * (dnorm[...] - shift_mean - pre[...] * gain_mean)).astype(BF16)
    dpext[dp_rows(b), :] = dpre
    dp_core = remote(dpext.at[dp_rows(b)], dpext.at[dp_rows(b)], dp_sem, 0, "br", core_peer)
    dp_y = remote(dpext.at[dp_rows(b)], dpext.at[dp_rows(b)], dp_sem, 1, "br", y_peer)
    dp_on = remote(dpext.at[dp_rows(y_peer)], dpext.at[dp_rows(y_peer)], dp_sem, 2, "br", core_peer)
    dp_x = remote(dpext.at[dp_rows(b)], dpext2.at[dp_rows(b)], dp2_sem, 0, "pix", x_peer)
    pending.extend([dp_core, dp_y, dp_on, dp_x])
    dp_x.start()
    dp_core.start()
    dp_y.start()
    edge_copies = []
    for at in range(B):
        down = pltpu.make_async_remote_copy(
            src_ref=dpext.at[pl.ds(PX, W)], dst_ref=dpext.at[pl.ds(0, W)], send_sem=dphalo_sem.at[0, at],
            recv_sem=dphalo_sem.at[1, 0], device_id={"pix": lax.rem(p + 1, P), "br": at}, device_id_type=MESH,
        )
        up = pltpu.make_async_remote_copy(
            src_ref=dpext.at[pl.ds(W, W)], dst_ref=dpext.at[pl.ds(W + PX, W)], send_sem=dphalo_sem.at[0, at],
            recv_sem=dphalo_sem.at[1, 1], device_id={"pix": lax.rem(p + P - 1, P), "br": at}, device_id_type=MESH,
        )
        edge_copies.append((down, up))
    far_copies = []
    for at in range(B):
        down = pltpu.make_async_remote_copy(
            src_ref=dpext.at[pl.ds(PX, W)], dst_ref=dpext2.at[pl.ds(0, W)], send_sem=dphalo2_sem.at[0, at],
            recv_sem=dphalo2_sem.at[1, 0], device_id={"pix": lax.rem(p + 2, P), "br": at}, device_id_type=MESH,
        )
        up = pltpu.make_async_remote_copy(
            src_ref=dpext.at[pl.ds(W, W)], dst_ref=dpext2.at[pl.ds(W + PX, W)], send_sem=dphalo2_sem.at[0, at],
            recv_sem=dphalo2_sem.at[1, 0], device_id={"pix": lax.rem(p + P - 2, P), "br": at}, device_id_type=MESH,
        )
        far_copies.append((down, up))
    sends_far_down = (b == B - 1) & (x_at == 1) & (p < P - 2)
    sends_far_up = (b == 0) & (x_at == 0) & (p > 1)

    @pl.when(sends_far_down)
    def _():
        for down, up in far_copies:
            down.start()

    @pl.when(sends_far_up)
    def _():
        for down, up in far_copies:
            up.start()


    @pl.when((b == B - 1) & (p < P - 1))
    def _():
        for down, up in edge_copies:
            down.start()

    @pl.when((b == 0) & (p > 0))
    def _():
        for down, up in edge_copies:
            up.start()

    @pl.when(p == 0)
    def _():
        dpext[pl.ds(0, W), :] = jnp.zeros((W, C), BF16)

    @pl.when(p == P - 1)
    def _():
        dpext[pl.ds(W + PX, W), :] = jnp.zeros((W, C), BF16)


    for peer, copy in fc_copies:

        @pl.when(peer > p)
        def _(copy=copy):
            copy.start()

    def half_block(at, half):
        return pl.ds(pl.multiple_of(W + at * OPX + half * (OPX // 2), 32), OPX // 2)

    dp2_core = remote(dpext2.at[dp_rows(b)], dpext2.at[dp_rows(b)], dp2_sem, 1, "br", core_peer)
    dp2_x = remote(dpext.at[half_block(y_peer, 0)], dpext2.at[half_block(y_peer, 0)], dp2_sem, 2, "pix", x_peer)
    dp2_y = remote(dpext2.at[half_block(b, 1)], dpext2.at[half_block(b, 1)], dp2_sem, 3, "br", y_peer)
    dp2_on = [
        remote(dpext2.at[half_block(y_peer, n)], dpext2.at[half_block(y_peer, n)], dp2_sem, 4 + n, "br", core_peer)
        for n in range(2)
    ]
    pending.extend([dp2_core, dp2_x, dp2_y] + dp2_on)
    dp_x.wait_recv()
    dp2_y.start()
    dp2_core.start()
    dp_y.wait_recv()
    dp2_x.start()
    dp_on.start()

    cq = C // B

    def cq_lanes(at):
        return pl.ds(pl.multiple_of(at * cq, cq), cq)

    cw_copies1 = exchange(
        "br", cw_sem1, lambda q: cwsend.at[:, cq_lanes(q)], lambda me: cwr1.at[me]
    )
    cwr1[b] = cwsend[:, cq_lanes(b)]
    pending.extend(cw_copies1)

    dp_core.wait_recv()
    dp_on.wait_recv()

    @pl.when(p > 0)
    def _():
        edge_copies[0][0].wait_recv()

    @pl.when(p < P - 1)
    def _():
        edge_copies[0][1].wait_recv()

    loads["xt"].wait()
    own_columns = xt[h_rows(b), :]
    for at in range(B):
        drecv[at * per : (at + 1) * per, :] = dot(own_columns, dpext[W + at * OPX : W + (at + 1) * OPX, :]).astype(BF16)
    cols = []
    for dx in range(3):
        cols.append(
            jnp.concatenate(
                [drecv[at * per + dx * block : at * per + (dx + 1) * block, :] for at in range(B)], axis=0
            )
        )
    parts = []
    for dy in range(3):
        part = dot_nt(cols[0], twu[dy]) + dot_nt(cols[1], twu[3 + dy]) + dot_nt(cols[2], twu[6 + dy])
        if dy != 1:
            mask = jnp.concatenate(
                [mgrp[dy // 2, 8 * at : 8 * at + 8, :] for at in range(B) for j in range(J)], axis=0
            )
            part = part * jnp.concatenate([mask] * (C // 128), axis=1)
        if dy > 0:
            part = pltpu.roll(part, dy, 0)
        parts.append(part)
    d_mix = parts[0] + parts[1] + parts[2]

    def group_rows(value, j):
        return jnp.concatenate(
            [value[(at * J + j) * 8 : (at * J + j) * 8 + 8] for at in range(B)], axis=0
        )

    for k in range(P // 2):
        value = d_mix[:, 128 * k : 128 * (k + 1)]
        for jj in range(HJ):
            left, right = group_rows(value, jj), group_rows(value, jj + HJ)
            for odd in range(2):
                at = 32 * (2 * k + odd)
                drsend[at : at + 32, 128 * jj : 128 * (jj + 1)] = pack(left, right, odd).astype(BF16)
    dr_copies = exchange("pix", dr_sem, lambda q: drsend.at[rm_rows(q)], lambda me: drrecv.at[rm_rows(me)])
    drrecv[rm_rows(p), :] = drsend[rm_rows(p), :]
    pending.extend(dr_copies)

    def o_lanes(at):
        return pl.ds(at * 128, 128)

    def from_all(ref, sem, sources):
        for src in sources:

            @pl.when(p != src)
            def _(src=src):
                pltpu.make_async_remote_copy(
                    src_ref=ref.at[0], dst_ref=ref.at[src], send_sem=sem.at[0, 0],
                    recv_sem=sem.at[1, src], device_id={"pix": p}, device_id_type=MESH,
                ).wait_recv()

    dw_copies = to_owners(lambda at: drecv.at[:, o_lanes(at)], dwrecv, dw_sem, only_before=True)

    shift_rows(dpext, mrow, backward_lanes)
    half_rows = C // 4

    def tap_product(tap, first):
        dy, dx = lax.div(tap, 3), lax.rem(tap, 3)
        return dot(fgrp[dx, first : first + half_c, 0:PX], shifted[:, pl.ds(pl.multiple_of((2 - dy) * C, C), C)])

    def own_step(tap, carry):
        keep[tap] = tap_product(tap, 0)
        return carry

    lax.fori_loop(0, 5, own_step, 0)
    dp2_x.wait_recv()
    dp2_on[0].start()
    dp2_y.wait_recv()
    dp2_on[1].start()
    lax.fori_loop(5, 9, own_step, 0)

    arrive(cw_copies1)
    cw2[...] = cwr1[0] + cwr1[1] + cwr1[2] + cwr1[3]
    c_part = cwsend.shape[0] // P

    def cw_rows(at):
        return pl.ds(pl.multiple_of(at * c_part, 8), c_part)

    cw_copies2 = exchange("pix", cw_sem2, lambda q: cw2.at[cw_rows(q)], lambda me: cwr2.at[me])
    cwr2[p] = cw2[cw_rows(p), :]
    pending.extend(cw_copies2)

    arrive(dr_copies)
    d_active = jnp.dot(mix_t[...], drrecv[...].astype(F32), precision=HIGH, preferred_element_type=F32)
    hat = bhat[...]
    d_normed = d_active * valid_f * gelu_parts(bnorm[...])[1]
    gain_part = over_bins(d_normed * hat)
    shift_part = over_bins(d_normed)
    scale = thrice(own_channels(bgain) * binv[0:1])
    d_pooled = scale * (d_normed - thrice(shift_part / total_bins) - hat * thrice(gain_part / total_bins)) * valid_f
    dssend[...] = (d_pooled / count).astype(BF16)
    dsrecv[p] = dssend[...]
    ds_copies = []
    for step in range(1, P // 2):
        copy = remote(dssend, dsrecv.at[p], ds_sem, step - 1, "pix", lax.rem(p + 2 * step, P))
        copy.start()
        ds_copies.append(copy)
    ds_across = []
    for step in range(P // 2):
        at = lax.rem(p + P - 2 * step, P)
        ds_across.append(remote(dsrecv.at[at], dsrecv.at[at], ds_sem, P // 2 - 1 + step, "pix", x_peer))
    ds_across[0].start()
    small = jnp.concatenate([gain_part, shift_part, jnp.zeros((6, 128), F32)], axis=0)
    smsend[...] = small
    sm_copies = exchange("pix", sm_sem, lambda q: smsend, lambda me: smrecv.at[me])
    smrecv[p] = small
    pending.extend(ds_copies + ds_across + sm_copies)

    in_column_order(dw_copies, lambda at: jnp.logical_not(owner_before(at)))

    @pl.when(x_at == 0)
    def _():
        dpext2[pl.ds(0, W), :] = dpext[pl.ds(PX, W), :]

    @pl.when(x_at == 1)
    def _():
        dpext2[pl.ds(W + PX, W), :] = dpext[pl.ds(W, W), :]

    @pl.when(p == 1)
    def _():
        dpext2[pl.ds(0, W), :] = jnp.zeros((W, C), BF16)

    @pl.when(p == P - 2)
    def _():
        dpext2[pl.ds(W + PX, W), :] = jnp.zeros((W, C), BF16)

    @pl.when((x_at == 1) & (p > 1))
    def _():
        far_copies[0][0].wait_recv()

    @pl.when((x_at == 0) & (p < P - 2))
    def _():
        far_copies[0][1].wait_recv()

    dp2_core.wait_recv()
    arrive(dp2_on)
    shift_rows(dpext2, mrow2, backward_lanes)

    def half_of(half):
        return pl.ds(half * half_rows, half_rows)

    def z_copy(tap, half):
        rows = half_of(half)
        return remote(
            sendx.at[tap, rows], recvz.at[tap, rows], zz_sem, tap * 2 + half, "pix", lax.rem(p + P - 2, P)
        )

    def a_rows(tap):
        return pl.ds(pl.multiple_of(lax.rem(tap, 3) * half_rows, 128), half_rows)

    def a_copy(tap):
        rows = pl.ds(pl.multiple_of((1 - z_at) * half_rows, 128), half_rows)
        return remote(sendx.at[tap, rows], pfrecv.at[lax.div(tap, 3), a_rows(tap)], a_sem, tap, "pix", lax.rem(p + 2 - 4 * z_at + 2 * P, P))

    def twg_copy(tap):
        return pltpu.make_async_copy(recvz.at[tap, half_of(0)], twg_hbm.at[tap], twg_sem.at[tap])

    def finish(tap):
        a_copy(tap).wait_recv()
        rows = pl.ds(pl.multiple_of(z_at * half_rows, 128), half_rows)
        recvz[tap, 0:half_rows, :] = (
            keep[tap, rows, :] + pfrecv[lax.div(tap, 3), a_rows(tap), :].astype(F32)
        ).astype(BF16)

    def peer_step(tap, carry):
        keep[tap] = keep[tap] + tap_product(tap, half_c)

        @pl.when((z_at == 0) | (z_at == 3))
        def _():
            sendx[tap] = keep[tap].astype(BF16)

        @pl.when(z_at == 3)
        def _():
            z_copy(tap, 0).start()
            z_copy(tap, 1).start()

        @pl.when(z_at == 0)
        def _():
            a_copy(tap).start()

        return carry

    lax.fori_loop(0, 9, peer_step, 0)

    def chain_step(tap, carry):
        @pl.when((z_at == 1) | (z_at == 2))
        def _():
            for half in range(2):
                z_copy(tap, half).wait_recv()
                rows = half_of(half)
                keep[tap, rows, :] = keep[tap, rows, :] + recvz[tap, rows, :].astype(F32)
                if half == 0:
                    sendx[tap, rows, :] = keep[tap, rows, :].astype(BF16)

                    @pl.when(z_at == 2)
                    def _():
                        z_copy(tap, 0).start()

                    @pl.when(z_at == 1)
                    def _():
                        a_copy(tap).start()

                else:

                    @pl.when(z_at == 2)
                    def _():
                        sendx[tap, rows, :] = keep[tap, rows, :].astype(BF16)
                        z_copy(tap, 1).start()

        return carry

    def chain_to(tap):
        lax.fori_loop(tap, tap + 1, chain_step, 0)

    chain_to(0)
    for step in range(1, P // 2):
        ds_copies[step - 1].wait_recv()
        ds_across[step].start()


    def unpack_all(source, target):
        for k in range(P // 2):
            even = source[2 * k].astype(F32)
            odd = source[2 * k + 1].astype(F32)
            for jj in range(HJ):
                lanes = slice(128 * jj, 128 * (jj + 1))
                halves = unpack(even[:, lanes], odd[:, lanes])
                for half in range(2):
                    j = jj + half * HJ
                    target[j * NB : (j + 1) * NB, 128 * k : 128 * (k + 1)] = halves[half].astype(BF16)

    arrive(cw_copies2)
    value = cwr2[0]
    for at in range(1, P):
        value = value + cwr2[at]
    cw3[...] = value
    cw_copies3 = exchange("pix", cw_sem3, lambda q: cw3, lambda me: cwr3.at[cw_rows(me)])
    cwr3[cw_rows(p), :] = value
    pending.extend(cw_copies3)

    chain_to(1)
    arrive(ds_across)
    unpack_all(dsrecv, ds_all)
    hot_mine = hot_own[...].astype(BF16)
    d_col = [dot(hot_mine, ds_all[j * NB : (j + 1) * NB, :]) for j in range(J)]
    d_col = jnp.concatenate(
        [d_col[j][8 * g : 8 * g + 8] for g in range(groups) for j in range(J)], axis=0
    ).astype(BF16)
    esend[...] = dot_nt(d_col, wb[...]).astype(BF16)

    def e_lanes(at):
        return pl.ds(pl.multiple_of(at * C, C), C)

    e_copies = exchange("br", e_sem, lambda q: esend.at[:, e_lanes(q)], lambda me: erecv.at[me])
    erecv[b] = esend[:, e_lanes(b)]
    pending.extend(e_copies)

    chain_to(2)
    shift_rows(dpext, mrow, backward_lanes)
    def back_step(at, carry):
        fg[pf_rows(at), :] = conv_chunk(at, -1)
        return carry

    lax.fori_loop(0, B // 2, back_step, 0)
    chain_to(3)
    lax.fori_loop(B // 2, B, back_step, 0)
    chain_to(4)
    for copy in pf_copies + h_copies:
        copy.wait_send()
    up_copies = []
    up_rows = 9 * 128
    for at in range(4):
        target = P // 2 + at
        up_copies.append(
            pltpu.make_async_remote_copy(
                src_ref=upsend.at[pl.ds(at * up_rows, up_rows)], dst_ref=uprecv.at[lax.rem(p, P // 2)], send_sem=up_sem.at[0, at],
                recv_sem=up_sem.at[1, p], device_id={"pix": target}, device_id_type=MESH,
            )
        )

    @pl.when(z_at >= 2)
    def _():
        from_all(actrecv, act_sem, range(P))
        unpack_all(actrecv, hsend)
        from_all(dwrecv, dw_sem, range(P))
        k_rows = P * B * block
        for dx in range(3):
            value = jnp.concatenate(
                [
                    dwrecv[at, per * owner + block * dx : per * owner + block * (dx + 1), :]
                    for at in range(P)
                    for owner in range(B)
                ],
                axis=0,
            )
            value = turned(value)
            for part in range(k_rows // C):
                pfsend[part, 128 * dx : 128 * (dx + 1), :] = value[:, C * part : C * (part + 1)]
        t_grp, k_grp = halo_rows((8 * B * P, 1), 0, 0)
        here_grp = jnp.where(k_grp < Q, row_info(t_grp)[0], -3)

        def up_step(dy, carry):
            mix = row_mix(t_grp + (dy - 1), g_row, i_row, here_grp)
            mix_high = mix.astype(BF16)
            mix_low = (mix - mix_high.astype(F32)).astype(BF16)
            for pair in range(J // 2):
                two = []
                for j in (2 * pair, 2 * pair + 1):
                    act = hsend[j * NB : (j + 1) * NB, :]
                    two.append(dot(mix_high, act) + dot(mix_low, act))
                for at in range(P * B):
                    value = jnp.concatenate([rows[8 * at : 8 * at + 8] for rows in two], axis=0)
                    to = at * block + 16 * pair
                    fgrp[to // C, to % C : to % C + 16, 0:C] = value.astype(BF16)
            total = None
            for part in range(k_rows // C):
                term = dot(pfsend[part], fgrp[part, 0:C, 0:C])
                total = term if total is None else total + term
            for at in range(4):
                upsend[pl.ds(pl.multiple_of(at * up_rows + dy * 384, 128), 384), :] = total[
                    :, 128 * at : 128 * (at + 1)
                ].astype(BF16)
            return carry

        lax.fori_loop(0, 3, up_step, 0)
        in_column_order(up_copies)
        for at in range(4):

            @pl.when(p == P // 2 + at)
            def _(at=at):
                uprecv[at] = upsend[at * up_rows : (at + 1) * up_rows, :]

    chain_to(5)
    arrive([copy for _, copy in fc_copies])
    hot16 = hot_all[...].astype(BF16)

    def eight(at, row):
        pair = fcrecv[at, row // 16 * 16 : row // 16 * 16 + 16, :].astype(F32)
        return pair[row % 16 : row % 16 + 8]

    for j in range(J):
        rows = jnp.concatenate(
            [eight(at, (g * J + j) * 8) for at in range(P) for g in range(groups)],
            axis=0,
        )
        fp_all[j * NB : (j + 1) * NB, :] = dot(hot16, rows.astype(BF16)).astype(BF16)
    fp_t[...] = turned(fp_all[...])

    bwg_out[...] = dot(fp_t[...], ds_all[...])
    arrive(sm_copies)
    for k in range(P // 2):
        lanes = slice(128 * k, 128 * (k + 1))
        is_low = low((1, 128))
        small_out[0:1, lanes] = jnp.where(is_low, smrecv[2 * k, 0:1, :], smrecv[2 * k + 1, 0:1, :])
        small_out[1:2, lanes] = jnp.where(is_low, smrecv[2 * k, 1:2, :], smrecv[2 * k + 1, 1:2, :])

    chain_to(6)
    arrive(e_copies)
    loads["spread"].wait()
    for g in range(groups):
        rows = jnp.concatenate([erecv[at, block * g : block * (g + 1), :] for at in range(B)], axis=0)
        total = fg[gpx * g : gpx * (g + 1), :] + dot(spread8[...], rows)
        shifted[gpx * g : gpx * (g + 1), 0:C] = total.astype(BF16)
    fg_copy = pltpu.make_async_copy(shifted.at[:, pl.ds(0, C)], fg_hbm, out_sem.at[0])
    fg_copy.start()

    chain_to(7)

    @pl.when(z_at < 2)
    def _():
        def most(tap, carry):
            finish(tap)
            twg_copy(tap).start()
            return carry

        lax.fori_loop(0, 7, most, 0)

    chain_to(8)

    @pl.when(z_at < 2)
    def _():
        def last(tap, carry):
            finish(tap)
            twg_copy(tap).start()
            return carry

        lax.fori_loop(7, 9, last, 0)

    @pl.when(z_at >= 2)
    def _():
        for src in range(4):

            @pl.when(p != P // 2 + src)
            def _(src=src):
                pltpu.make_async_remote_copy(
                    src_ref=upsend.at[pl.ds(0, up_rows)], dst_ref=uprecv.at[src], send_sem=up_sem.at[0, 0],
                    recv_sem=up_sem.at[1, P // 2 + src], device_id={"pix": p}, device_id_type=MESH,
                ).wait_recv()

        def gather(tap, carry):
            rows = pl.ds(pl.multiple_of(tap * 128, 128), 128)
            value = jnp.concatenate([uprecv[at, rows, :] for at in range(4)], axis=0)
            recvz[tap, 0:half_rows, :] = turned(value)
            twg_copy(tap).start()
            return carry

        lax.fori_loop(0, 9, gather, 0)

    arrive(cw_copies3)
    cwg_out[...] = cwr3[0 : d.classes, :]

    pending.extend(fp_copies)

    for copy in pending:
        copy.wait_send()

    @pl.when(p < P - 1)
    def _():
        halo_down.wait_send()

    @pl.when(p > 0)
    def _():
        halo_up.wait_send()

    @pl.when((b == B - 1) & (p < P - 1))
    def _():
        for down, up in edge_copies:
            down.wait_send()

    @pl.when((b == 0) & (p > 0))
    def _():
        for down, up in edge_copies:
            up.wait_send()

    @pl.when(sends_far_down)
    def _():
        for down, up in far_copies:
            down.wait_send()

    @pl.when(sends_far_up)
    def _():
        for down, up in far_copies:
            up.wait_send()

    for at in range(4):

        @pl.when(p != P // 2 + at)
        def _(at=at):
            dw_copies[at].wait_send()
            act_copies[at].wait_send()

        @pl.when((z_at >= 2) & (p != P // 2 + at))
        def _(at=at):
            up_copies[at].wait_send()

    def sent(tap, carry):
        @pl.when(z_at >= 2)
        def _():
            z_copy(tap, 0).wait_send()
            z_copy(tap, 1).wait_send()

        @pl.when(z_at < 2)
        def _():
            a_copy(tap).wait_send()

        return carry

    lax.fori_loop(0, 9, sent, 0)
    fg_copy.wait()

    def handed(tap, carry):
        twg_copy(tap).wait()
        return carry

    lax.fori_loop(0, 9, handed, 0)


def spread_tables(width, own, rows):
    side = max(bin_sides)
    count = len(bin_sides)
    cols = shifted_columns(bin_sides, width, side)
    up = np.zeros((own, width, count, 3, side, 8), np.float32)
    for m in range(own):
        up[m, :, :, :, :, m] = cols.transpose(2, 0, 1, 3)
    up = up.reshape(own * width, count * 3 * side * 8)
    bins = column_bins(bin_sides, width, side)
    pool = np.zeros((count, side, 8, 8, width), np.float32)
    spread = np.zeros((8, width, count, side, 8), np.float32)
    for r in range(8):
        pool[:, :, r, r, :] = bins
        spread[r, :, :, :, r] = bins.transpose(2, 0, 1)
    bf16 = jnp.bfloat16
    return (
        jnp.asarray(up, bf16),
        jnp.asarray(up.T, bf16),
        jnp.asarray(pool.reshape(count, side * 8, 8 * width), bf16),
        jnp.asarray(spread.reshape(8 * width, count * side * 8), bf16),
    )


def on_device_fused(
    features,
    branch_weight,
    branch_gain,
    branch_shift,
    trunk_weight,
    trunk_gain,
    trunk_shift,
    class_weight,
    class_bias,
    heights,
    logit_grad,
):
    P, B = lax.axis_size("pix"), lax.axis_size("br")
    d = Shape(features, branch_weight, class_weight, heights, P, B)
    W, C, J, NB, R, PX, OPX = d.width, d.ch, d.side, d.bins, d.rows, d.px, d.own_px
    CH, K = d.channels, d.classes
    per = 3 * J * 8
    groups = R // 8
    up, up_t, pool, spread = spread_tables(W, d.own, R)
    half = C // 4
    kp = -(-K // (8 * P)) * 8 * P
    vmem, sem = pltpu.VMEM, pltpu.SemaphoreType.DMA
    scratch = dict(
        fext=vmem((PX + 2 * W, C), BF16), shifted=vmem((PX, 3 * C), BF16), fgrp=vmem((groups, 8 * W, CH), BF16),
        wb=vmem((CH, C), BF16), twf=vmem((9, C, C), BF16), twu=vmem((9, C, C), BF16),
        xc=vmem(up.shape, BF16), xt=vmem(up_t.shape, BF16), pool8=vmem(pool.shape[1:], BF16), spread8=vmem(spread.shape, BF16),
        fc_hi=vmem((groups * J * 8, CH), BF16), zsend=vmem((P, R, 384), F32), zrecv=vmem((P * R, 384), F32),
        fcrecv=vmem((P, groups * J * 8, CH // P), BF16), pfsend=vmem((B - 1, OPX, C), BF16), pfrecv=vmem((B - 1, OPX, C), BF16),
        hidden=vmem((OPX, C), BF16),
        hot_all=vmem((NB, P * R), F32), mix_all=vmem((8 * B * P, NB), F32), mix_t=vmem((NB, 8 * B * P), F32), hot_own=vmem((R, NB), F32),
        mrow=vmem((2, 32, 128), F32), mrow2=vmem((2, 32, 128), F32), mgrp=vmem((2, 8 * B, 128), F32),
        bhat=vmem((NB, 384), F32), bnorm=vmem((NB, 384), F32), binv=vmem((8, 128), F32),
        rmsend=vmem((8 * B * P, 384), BF16), rmrecv=vmem((8 * B * P, 384), BF16), actsend=vmem((NB, 384), BF16), actrecv=vmem((P, NB, 384), BF16),
        hsend=vmem((B * per, C), BF16), hrecv=vmem((B * per, C), BF16),
        st1=vmem((8, 128), F32), st2=vmem((8, 128), F32), st3=vmem((16, 128), F32), st4=vmem((16, 128), F32),
        sr1=vmem((B, 8, 128), F32), sr2=vmem((P, 8, 128), F32), sr3=vmem((B, 16, 128), F32), sr4=vmem((P, 16, 128), F32), tot=vmem((16, 128), F32),
        cwp=vmem((256, C), BF16), lgp=vmem((OPX, 256), BF16), cwsend=vmem((kp, C), F32), cwr1=vmem((B, kp, C // B), F32),
        cw2=vmem((kp, C // B), F32), cwr2=vmem((P, kp // P, C // B), F32), cw3=vmem((kp // P, C // B), F32), cwr3=vmem((kp, C // B), F32),
        dpext=vmem((PX + 2 * W, C), BF16), dpext2=vmem((PX + 2 * W, C), BF16), drecv=vmem((B * per, C), BF16),
        drsend=vmem((8 * B * P, 384), BF16), drrecv=vmem((8 * B * P, 384), BF16),
        dwrecv=vmem((P, B * per, 128), BF16),
        dssend=vmem((NB, 384), BF16), dsrecv=vmem((P, NB, 384), BF16), smsend=vmem((8, 128), F32), smrecv=vmem((P, 8, 128), F32),
        ds_all=vmem((J * NB, C), BF16), fp_all=vmem((J * NB, CH // P), BF16), fp_t=vmem((CH // P, J * NB), BF16), esend=vmem((groups * J * 8, CH), BF16),
        erecv=vmem((B, groups * J * 8, C), BF16), fg=vmem((PX, C), F32), keep=vmem((9, 2 * half, C), F32),
        sendx=vmem((9, 2 * half, C), BF16),
        recvz=vmem((9, 2 * half, C), BF16),
        upsend=vmem((4 * 9 * 128, 128), BF16), uprecv=vmem((4, 9 * 128, 128), BF16), eye=vmem((C, C), BF16),
        load_sem=sem((27,)), out_sem=sem((2,)), twg_sem=sem((9,)), halo_sem=sem((2, 2)), z_sem=sem((2, P)), fc_sem=sem((2, P)), pf_sem=sem((2, B)),
        rm_sem=sem((2, P)), act_sem=sem((2, P)), h_sem=sem((2, B)),
        st_sem1=sem((2, B)), st_sem2=sem((2, P)), st_sem3=sem((2, B)), st_sem4=sem((2, P)),
        cw_sem1=sem((2, B)), cw_sem2=sem((2, P)), cw_sem3=sem((2, P)),
        dp_sem=sem((2, B)), dphalo_sem=sem((2, B)), dp2_sem=sem((2, 6)), dphalo2_sem=sem((2, B)), fp_sem=sem((2, 2)), dr_sem=sem((2, P)), dw_sem=sem((2, P)), ds_sem=sem((2, P)),
        sm_sem=sem((2, P)), e_sem=sem((2, B)), zz_sem=sem((2, 24)), a_sem=sem((2, 9)), up_sem=sem((2, P)),
    )
    hbm = pl.BlockSpec(memory_space=pl.ANY)
    local = pl.BlockSpec(memory_space=pltpu.VMEM)
    scalars = pl.BlockSpec(memory_space=pltpu.SMEM)

    def out(shape, dtype):
        return jax.ShapeDtypeStruct(shape, dtype)

    outs = pl.pallas_call(
        functools.partial(fused_kernel, d),
        out_shape=(
            out((OPX, K), BF16), out((PX, C), BF16), out((CH // P, C), F32), out((9, half, C), BF16),
            out((K, C // B), F32), out((8, C), F32),
        ),
        in_specs=[hbm] * 7 + [local] * 7 + [scalars],
        out_specs=(local, hbm, local, hbm, local, local),
        scratch_shapes=list(scratch.values()),
        compiler_params=pltpu.CompilerParams(
            collective_id=0, has_side_effects=True, vmem_limit_bytes=127 * 512 * 1024
        ),
    )(
        features.reshape(PX, CH), branch_weight[0], trunk_weight.reshape(9, 2 * C, C), up, up_t, pool, spread,
        branch_gain, branch_shift, trunk_gain[None], trunk_shift[None], class_weight.T, class_bias[None],
        logit_grad.reshape(OPX, K), heights,
    )

    def hand_on(*refs):
        src, small, dst, smalls = refs[:5], refs[5], refs[6:11], refs[11:16]
        held, wide, sems = refs[16:21], {1: refs[21], 3: refs[22]}, refs[23]
        parts = []
        for at in (1, 3, 0, 2, 4):
            rows = src[at].shape[0]
            cuts = {1: 8, 3: 9}.get(at, 1)
            for cut in range(cuts):
                part = pl.ds(cut * (rows // cuts), rows // cuts)
                n = len(parts)
                parts.append(
                    (
                        at,
                        part,
                        pltpu.make_async_copy(src[at].at[part], held[at].at[part], sems.at[0, n]),
                        pltpu.make_async_copy(wide.get(at, held[at]).at[part], dst[at].at[part], sems.at[1, n]),
                    )
                )
        for _, _, there, _ in parts:
            there.start()
        for at, ref in enumerate(smalls):
            ref[...] = small[at : at + 1, 0 : ref.shape[1]]
        for at, part, there, back in parts:
            there.wait()
            if at in wide:
                wide[at][part] = held[at][part].astype(F32)
            back.start()
        for _, _, _, back in parts:
            back.wait()

    logits, fg, bwg, twg, cwg, bgg, bsg, tgg, tsg, cbg = pl.pallas_call(
        hand_on,
        out_shape=tuple(out(o.shape, BF16 if at == 0 else F32) for at, o in enumerate(outs[:5]))
        + tuple(out((1, n), F32) for n in (C, C, C // B, C // B, K)),
        in_specs=[hbm] * 5 + [local],
        out_specs=tuple([hbm] * 5 + [local] * 5),
        scratch_shapes=[vmem(o.shape, o.dtype) for o in outs[:5]]
        + [vmem(outs[1].shape, F32), vmem(outs[3].shape, F32), sem((2, 24))],
        compiler_params=pltpu.CompilerParams(vmem_limit_bytes=127 * 512 * 1024),
    )(*outs)
    return (
        logits.reshape(d.own, W, K), fg.reshape(R, W, C), bwg[None], bgg, bsg,
        twg.reshape(1, 3, 3, half, C), tgg[0], tsg[0], cwg.T, cbg[0],
    )


def solution(mesh):
    in_specs = (
        P("pix", None, None),
        P("br", None, None),
        P("br", None),
        P("br", None),
        P("br", None, None, None, None),
        P(),
        P(),
        P(),
        P(),
        P(),
        P(("pix", "br"), None, None),
    )
    out_specs = (
        P(("pix", "br"), None, None),
        P("pix", None, "br"),
        P("br", "pix", None),
        P("br", None),
        P("br", None),
        P("br", None, None, "pix", None),
        P("br"),
        P("br"),
        P("br", None),
        P(),
    )
    fused = mesh.shape["pix"] == 8 and mesh.shape["br"] == 4
    return jax.shard_map(
        on_device_fused if fused else on_device, mesh=mesh, in_specs=in_specs, out_specs=out_specs, check_vma=False
    )
```
